32 devices in a mesh: expert: 8 (over z, y), section: 4 (over x, core).
Axes of the slice: x: 2, y: 2, z: 4, core: 2. Of those that a mesh axis runs over, the one named last changes fastest.
Arguments:
- section_acts: bfloat16 [4, 1536, 2048], P('section', 'expert'), may hold values from -6 to 6
- section_input_gradients: bfloat16 [4, 1536, 2048], P('section', 'expert'), may hold values from -6 to 6
- saved_input: bfloat16 [4, 1536, 2048], P('section', 'expert'), may hold values from -6 to 6
- fwd_routes: int32 [4, 768, 8], P('section'), may hold values from 0 to 255, all different within a row; in each aligned block of 192 rows (0 to 191, 192 to 383, ..., all dimensions but the last counted through in order) at most 12 rows name the same one
- fwd_probs: float32 [4, 768, 8], P('section'), may hold values from 0.1 to 1
- back_routes: int32 [4, 768, 8], P('section'), may hold values from 0 to 255, all different within a row; in each aligned block of 192 rows (0 to 191, 192 to 383, ..., all dimensions but the last counted through in order) at most 12 rows name the same one
- back_probs: float32 [4, 768, 8], P('section'), may hold values from 0.1 to 1
- w_gate: bfloat16 [4, 8192, 4096], P('section', 'expert'), may hold values from -0.09375 to 0.09375
- w_up: bfloat16 [4, 8192, 4096], P('section', 'expert'), may hold values from -0.09375 to 0.09375
- w_down: bfloat16 [4, 8192, 4096], P('section', 'expert'), may hold values from -0.125 to 0.125
Outputs:
- section_out: bfloat16 [4, 1536, 2048], P('section', 'expert')
- input_grads: bfloat16 [4, 1536, 2048], P('section', 'expert')
The draws below stay inside these ranges and needn't reach their ends.
Inputs may be any that keep to these rules, and one draw needn't show every extreme that they name: `fwd_routes`: in each aligned block of 192 rows (one group of one section) no id is named by more than 12 rows, and some block has an id named by exactly 12; every id is named somewhere. `back_routes`: in each aligned block of 192 rows (one group of one section) no id is named by more than 12 rows, and some block has an id named by exactly 12; every id is named somewhere.
All inputs are finite; a program needn't handle non-finite values.
Results may differ from the reference program's by a relative error of at most 0.0075.
Values may be sent and summed in bfloat16 or wider, within the bound.
No kernel may reach another device: no remote copies, remote signals or barrier semaphores. Data moves between devices by JAX's collectives and lax.ppermute only.
A program may use at most 64 MiB of HBM per device.

```python
import math
import jax
import jax.numpy as jnp
import numpy as np
from jax import lax

D = 4096
F = 2048
N_ROUTED = 256
TOP = 8
E_WIN = 4
TOK_G = 192
DS = 2048
CAP = 12
TOKENS = 768
ROWS = 1536
FW = 8192
N_EXPERT = 8
N_SECTION = 4


def levels(key, extent, cuts, least, high):
    def one(axis_at, blocks):
        draws = jax.random.uniform(jax.random.fold_in(jax.random.fold_in(key, 6), axis_at), (blocks,), jnp.float32, least / len(cuts), high / len(cuts))
        return jnp.repeat(jnp.exp(draws), extent[axis_at] // blocks).reshape((-1,) + (1,) * (len(extent) - axis_at - 1))

    loudness = one(*cuts[0])
    for cut in cuts[1:]:
        loudness = loudness * one(*cut)
    return loudness


def deal_out(key, own, number, rows, number_of, top, bound, skew):
    order = jax.random.permutation(key, number_of)
    heavy_load, ordinary = load_shares(number_of, rows * top, bound, skew, True), load_shares(number_of, rows * top, bound, skew, False)
    places = jnp.arange(number_of)

    def named(lengths, turn):
        used = int((lengths > 0).sum())
        fixed = max(1, used // 4)
        moved = fixed + (places - fixed + turn * (used - fixed)) % max(1, number_of - fixed)
        return jnp.zeros((number_of,), jnp.int32).at[order[jnp.where(places < fixed, places, moved)]].set(jnp.asarray(lengths, jnp.int32))

    lengths = jnp.where(number % 4 == 0, named(heavy_load, number // 4), named(ordinary, number - number // 4 - 1))
    mixed = jax.random.permutation(jax.random.fold_in(own, 3), number_of)
    donor, taker = mixed[0:number_of // 2 * 2:2], mixed[1:number_of // 2 * 2:2]
    room = jnp.minimum(lengths[donor] - 1, bound - lengths[taker]) // 2
    room = jnp.where((donor == order[0]) | (taker == order[0]) | (lengths[taker] == 0), 0, jnp.maximum(room, 0))
    moved = jax.random.randint(jax.random.fold_in(own, 4), (number_of // 2,), 0, 1 << 20) % (room + 1)
    lengths = lengths.at[donor].add(-moved).at[taker].add(moved)
    items = jnp.searchsorted(jnp.cumsum(lengths), jnp.arange(rows * top), side="right").astype(jnp.int32)
    grid = items.reshape(top, rows).T
    grid = grid[jax.random.permutation(jax.random.fold_in(own, 1), rows)]
    turn = jax.random.randint(jax.random.fold_in(own, 2), (rows, 1), 0, top)
    return jnp.take_along_axis(grid, (jnp.arange(top)[None, :] + turn) % top, axis=1)


def load_shares(count, total, limit, lean, full):
    weights = [(1 << 20) // math.isqrt(standing ** lean) + 1 for standing in range(1, count + 1)]
    largest = limit if full else min(limit, max(-(-total // count), total * weights[0] // sum(weights)))
    least = 1 if total - largest >= count - 1 else 0
    given, rest = [largest] + [least] * (count - 1), total - largest - least * (count - 1)
    while rest > 0:
        candidates = [i for i in range(1, count) if given[i] < largest] or [i for i in range(1, count) if given[i] < limit]
        mass, budget = sum([weights[i] for i in candidates]), rest
        for i in candidates:
            extra = min(limit - given[i], max(1, budget * weights[i] // mass), rest)
            given[i] = given[i] + extra
            rest = rest - extra
    return np.array(given)


def noise(own_key, shape, spread, most, shards=(), held_as=jnp.bfloat16):
    result = spread * jax.random.normal(own_key, shape, jnp.float32)
    if shards:
        result = result * levels(own_key, shape, shards, -0.22, 0.18)
    return jnp.clip(result, -most, most).astype(held_as)


def setup_inputs(seed: int = 0) -> dict:
    key_list = jax.random.split(jax.random.key(seed), 11)
    section_acts = noise(key_list[0], (N_SECTION, ROWS, DS), 1.0, 6.0, ((0, 4), (1, 8)))
    section_input_gradients = noise(key_list[1], (N_SECTION, ROWS, DS), 1.0, 6.0, ((0, 4), (1, 8)))
    saved_input = noise(key_list[2], (N_SECTION, ROWS, DS), 1.0, 6.0, ((0, 4), (1, 8)))
    fwd_routes_keys = jax.random.split(jax.random.fold_in(key_list[3], 1), N_SECTION * TOKENS // TOK_G)
    fwd_routes_turns = jax.random.permutation(jax.random.fold_in(key_list[3], 3), N_SECTION * TOKENS // TOK_G)
    fwd_routes = jax.vmap(lambda own, number: deal_out(jax.random.fold_in(key_list[3], 2), own, number, TOK_G, N_ROUTED, TOP, CAP, 2))(fwd_routes_keys, fwd_routes_turns).reshape((N_SECTION, TOKENS, TOP))
    fwd_probs = jnp.clip(jnp.exp(math.log(1.0) - 2.3025851 * jax.random.uniform(key_list[4], (N_SECTION, TOKENS, TOP), jnp.float32) ** levels(key_list[4], (N_SECTION, TOKENS, TOP), ((0, 4),), -0.2, 0.2)), 0.1, 1.0)
    back_routes_keys = jax.random.split(jax.random.fold_in(key_list[5], 1), N_SECTION * TOKENS // TOK_G)
    back_routes_turns = jax.random.permutation(jax.random.fold_in(key_list[5], 3), N_SECTION * TOKENS // TOK_G)
    back_routes = jax.vmap(lambda own, number: deal_out(jax.random.fold_in(key_list[5], 2), own, number, TOK_G, N_ROUTED, TOP, CAP, 2))(back_routes_keys, back_routes_turns).reshape((N_SECTION, TOKENS, TOP))
    back_probs = jnp.clip(jnp.exp(math.log(1.0) - 2.3025851 * jax.random.uniform(key_list[6], (N_SECTION, TOKENS, TOP), jnp.float32) ** levels(key_list[6], (N_SECTION, TOKENS, TOP), ((0, 4),), -0.2, 0.2)), 0.1, 1.0)
    w_gate = noise(key_list[7], (N_SECTION, FW, D), D ** -0.5, 0.09375, ((0, 4), (1, 8)))
    w_up = noise(key_list[8], (N_SECTION, FW, D), D ** -0.5, 0.09375, ((0, 4), (1, 8)))
    w_down = noise(key_list[9], (N_SECTION, FW, D), F ** -0.5, 0.125, ((0, 4), (1, 8)))
    return {"section_acts": section_acts, "section_input_gradients": section_input_gradients, "saved_input": saved_input, "fwd_routes": fwd_routes, "fwd_probs": fwd_probs, "back_routes": back_routes, "back_probs": back_probs, "w_gate": w_gate, "w_up": w_up, "w_down": w_down}


def tables(block, gains):
    labels = jnp.arange(E_WIN, dtype=jnp.int32)
    hits = block[:, :, None] == labels[None, None, :]
    chosen = jnp.sum(hits.astype(jnp.int32), axis=1, dtype=jnp.int32)
    weight = jnp.sum(jnp.where(hits, gains[:, :, None], jnp.float32(0.0)), axis=1)
    before = jnp.cumsum(chosen, axis=0, dtype=jnp.int32) - chosen
    places = jnp.arange(CAP, dtype=jnp.int32)
    mask = (before[:, None, :] == places[None, :, None]) & (chosen[:, None, :] > 0)
    picker = mask.astype(jnp.float32).reshape(block.shape[0], CAP * E_WIN)
    weighted = jnp.where(mask, weight[:, None, :], jnp.float32(0.0)).reshape(block.shape[0], CAP * E_WIN)
    return picker, weighted


def reference(section_acts, section_input_gradients, saved_input, fwd_routes, fwd_probs, back_routes, back_probs, w_gate, w_up, w_down):
    split = N_EXPERT // E_WIN
    hid = F // split
    high = lax.Precision.HIGHEST

    def unblock(values_array):
        cols = values_array.shape[1]
        return values_array.reshape(E_WIN, split, TOK_G, cols).transpose(0, 2, 1, 3).reshape(E_WIN, TOK_G, split * cols)

    def regroup_blocks(values_array):
        cols = D // split
        return values_array.reshape(E_WIN, TOK_G, split, cols).transpose(0, 2, 1, 3).reshape(E_WIN * split * TOK_G, cols)

    def to_experts(rows):
        return rows.reshape(E_WIN, CAP, E_WIN, D).transpose(2, 0, 1, 3).reshape(E_WIN, E_WIN * CAP, D)

    def to_groups(rows):
        return rows.reshape(E_WIN, E_WIN, CAP, D).transpose(1, 2, 0, 3).reshape(E_WIN, CAP * E_WIN, D)

    def one_section(items):
        acts, grads, saved, f_routes, f_probs, b_routes, b_probs, gate_w, up_w, down_w = items
        x_in = unblock(acts)
        dy_in = unblock(grads)
        backward_input = unblock(saved)
        f_pick, f_weight = jax.vmap(tables)(f_routes.reshape(E_WIN, TOK_G, TOP), f_probs.reshape(E_WIN, TOK_G, TOP))
        b_pick, b_weight = jax.vmap(tables)(b_routes.reshape(E_WIN, TOK_G, TOP), b_probs.reshape(E_WIN, TOK_G, TOP))
        gate_e = gate_w.reshape(E_WIN, split, hid, D).astype(jnp.float32)
        up_e = up_w.reshape(E_WIN, split, hid, D).astype(jnp.float32)
        down_e = down_w.reshape(E_WIN, split, hid, D).astype(jnp.float32)

        f_rows = jnp.einsum('gtm,gtd->gmd', f_pick, x_in.astype(jnp.float32), precision=high).astype(jnp.bfloat16)
        f_rows = to_experts(f_rows).astype(jnp.float32)
        gate_pre = jnp.einsum('erd,eshd->ersh', f_rows, gate_e, precision=high)
        up_pre = jnp.einsum('erd,eshd->ersh', f_rows, up_e, precision=high)
        hidden = (jax.nn.silu(gate_pre) * up_pre).astype(jnp.bfloat16)
        part = jnp.einsum('ersh,eshd->esrd', hidden.astype(jnp.float32), down_e, precision=high).astype(jnp.bfloat16)
        made = jnp.sum(part.astype(jnp.float32), axis=1)
        moe = jnp.einsum('gtm,gmd->gtd', f_weight, to_groups(made), precision=high)
        layer_output = (x_in.astype(jnp.float32) + moe).astype(jnp.bfloat16)

        scale = jnp.sum(b_weight, axis=1)
        b_rows = jnp.einsum('gtm,gtd->gmd', b_pick, backward_input.astype(jnp.float32), precision=high).astype(jnp.bfloat16)
        g_rows = jnp.einsum('gtm,gtd->gmd', b_pick, dy_in.astype(jnp.float32), precision=high)
        g_rows = (g_rows * scale[:, :, None]).astype(jnp.bfloat16)
        b_rows = to_experts(b_rows).astype(jnp.float32)
        g_rows = to_experts(g_rows).astype(jnp.float32)
        gate_b = jnp.einsum('erd,eshd->ersh', b_rows, gate_e, precision=high)
        up_b = jnp.einsum('erd,eshd->ersh', b_rows, up_e, precision=high)
        sig = jax.nn.sigmoid(gate_b)
        act = gate_b * sig
        d_hidden = jnp.einsum('erd,eshd->ersh', g_rows, down_e, precision=high)
        d_up = (d_hidden * act).astype(jnp.bfloat16).astype(jnp.float32)
        d_gate = (d_hidden * up_b * sig * (1.0 + gate_b * (1.0 - sig))).astype(jnp.bfloat16).astype(jnp.float32)
        back = jnp.einsum('ersh,eshd->esrd', d_gate, gate_e, precision=high) + jnp.einsum('ersh,eshd->esrd', d_up, up_e, precision=high)
        back = jnp.sum(back.astype(jnp.bfloat16).astype(jnp.float32), axis=1)
        dx_moe = jnp.einsum('gtm,gmd->gtd', b_pick, to_groups(back), precision=high)
        input_gradient = (dy_in.astype(jnp.float32) + dx_moe).astype(jnp.bfloat16)
        return regroup_blocks(layer_output), regroup_blocks(input_gradient)

    acts_all = jnp.roll(section_acts, 1, axis=0)
    grads_all = jnp.roll(section_input_gradients, -1, axis=0)
    section_out, input_grads = lax.map(one_section, (acts_all, grads_all, saved_input, fwd_routes, fwd_probs, back_routes, back_probs, w_gate, w_up, w_down))
    return section_out, input_grads
```

```python
import functools
import jax
import jax.numpy as jnp
from jax import lax
from jax.experimental import pallas as pl
from jax.experimental.pallas import tpu as pltpu
from jax.sharding import PartitionSpec as P

N_ROUTED = 256
TOP = 8
E_WIN = 4
F32 = jnp.float32
BF16 = jnp.bfloat16
VMEM_LIMIT = 8 << 20


def mm(a, b, ca=1, cb=0, precision=None):
    dims = (((ca,), (cb,)), ((), ()))
    return lax.dot_general(a, b, dims, precision=precision, preferred_element_type=F32)


class Sizes:
    def __init__(self, count, width, hidden, split):
        self.count, self.width, self.hidden, self.split = count, width, hidden, split
        self.cap = count * TOP * 2 // N_ROUTED
        self.slots = E_WIN * self.cap
        self.parts = min(4, width // 128)
        self.cols = width // self.parts
        self.piece = self.parts * self.cap
        self.spread = E_WIN * self.piece


def place_of(sz, i):
    piece = sum([(i >= sz.piece * n).astype(jnp.int32) for n in range(1, E_WIN)])
    i = i - sz.piece * piece
    part = sum([(i >= sz.cap * n).astype(jnp.int32) for n in range(1, sz.parts)])
    return piece, part, i - sz.cap * part


def one_hot(mask):
    return jnp.where(mask, 1.0, 0.0).astype(BF16)


def route_masks(routes, probs, expert, place, earlier):
    chosen = jnp.zeros(expert.shape, F32)
    weight = jnp.zeros(expert.shape, F32)
    for c in range(TOP):
        hit = routes[c : c + 1, :] == expert
        chosen += jnp.where(hit, 1.0, 0.0)
        if probs is not None:
            weight += jnp.where(hit, probs[c : c + 1, :], 0.0)
    before = mm(chosen.astype(BF16), earlier)
    mask = (chosen > 0.5) & (jnp.abs(before - place.astype(F32)) < 0.5)
    return mask, weight


def my_group(ref, group, count):
    block = ref[:, :count]
    for n in range(1, E_WIN):
        block = jnp.where(group == n, ref[:, n * count : (n + 1) * count], block)
    return block


def earlier_tokens(sz):
    shape = (sz.count, sz.count)
    return one_hot(lax.broadcasted_iota(jnp.int32, shape, 0) < lax.broadcasted_iota(jnp.int32, shape, 1))


def piece_masks(sz, routes_ref, probs_ref):
    group = lax.axis_index("expert") // sz.split
    shape = (sz.spread, sz.count)
    piece, part, place = place_of(sz, lax.broadcasted_iota(jnp.int32, shape, 0))
    routes = my_group(routes_ref, group, sz.count)
    probs = None if probs_ref is None else my_group(probs_ref, group, sz.count)
    mask, weight = route_masks(routes, probs, piece ^ group, place, earlier_tokens(sz))
    return mask, weight, part


def pick(sz, mask, part, values):
    picked = jnp.zeros((sz.spread, sz.cols), F32)
    for q in range(sz.parts):
        picked += mm(one_hot(mask & (part == q)), values[:, q * sz.cols : (q + 1) * sz.cols])
    return picked


def put_pieces(sz, values, pieces):
    for o, piece in enumerate(pieces):
        piece[...] = values[o * sz.piece : (o + 1) * sz.piece].astype(BF16)


def fetch(pairs, sems):
    copies = [pltpu.make_async_copy(src, dst, sems.at[n]) for n, (src, dst) in enumerate(pairs)]
    for c in copies:
        c.start()
    return copies


def local_kernel(sz, fr, fp, br, bp, saved, w_f, w_b, *rest):
    pieces, (fr_v, fp_v, br_v, bp_v, saved_v, sems) = rest[:E_WIN], rest[E_WIN:]
    pairs = [(br, br_v), (bp, bp_v), (fr, fr_v), (fp, fp_v), (saved, saved_v)]
    copies = fetch(pairs, sems)
    for c in copies[:4]:
        c.wait()
    mask, _, part = piece_masks(sz, br_v, bp_v)
    w_b[...] = one_hot(mask)
    copies[4].wait()
    put_pieces(sz, pick(sz, mask, part, saved_v), pieces)
    mask, weight, _ = piece_masks(sz, fr_v, fp_v)
    w_f[...] = jnp.where(mask, weight, 0.0)


def pick_kernel(sz, br, bp, fr, grads, acts, after, *refs):
    g_out, x_out, (grads_v, acts_v, sems) = refs[:E_WIN], refs[E_WIN : 2 * E_WIN], refs[2 * E_WIN :]
    copies = fetch([(grads, grads_v), (acts, acts_v)], sems)
    g_mask, weight, part = piece_masks(sz, br, bp)
    scale = jnp.sum(jnp.where(g_mask, weight, 0.0), axis=1, keepdims=True)
    x_mask, _, _ = piece_masks(sz, fr, None)
    copies[0].wait()
    put_pieces(sz, pick(sz, g_mask, part, grads_v) * scale, g_out)
    copies[1].wait()
    put_pieces(sz, pick(sz, x_mask, part, acts_v), x_out)


def unpick(sz, cat, rows):
    shape = (sz.slots, sz.spread)
    slot = lax.broadcasted_iota(jnp.int32, shape, 0)
    piece, part, place = place_of(sz, lax.broadcasted_iota(jnp.int32, shape, 1))
    here = slot == piece * sz.cap + place
    for q in range(sz.parts):
        rows[:, q * sz.cols : (q + 1) * sz.cols] = mm(one_hot(here & (part == q)), cat).astype(BF16)


def unpick_kernel(sz, *refs):
    unpick(sz, jnp.concatenate([p[...] for p in refs[:E_WIN]], axis=0), refs[-1])


def fold_kernel(sz, *refs):
    slices, pieces = refs[: sz.split], refs[sz.split :]
    rows = slices[0][...].astype(F32)
    for s in slices[1:]:
        rows += s[...].astype(F32)
    rows = rows.astype(BF16)
    shape = (sz.spread, sz.slots)
    piece, part, place = place_of(sz, lax.broadcasted_iota(jnp.int32, shape, 0))
    here = lax.broadcasted_iota(jnp.int32, shape, 1) == piece * sz.cap + place
    out = jnp.zeros((sz.spread, sz.cols), F32)
    for q in range(sz.parts):
        out += mm(one_hot(here & (part == q)), rows[:, q * sz.cols : (q + 1) * sz.cols])
    put_pieces(sz, out, pieces)


def combine_kernel(sz, weighted, *refs):
    values, w, pieces, out = refs[0], refs[1], refs[2 : 2 + E_WIN], refs[2 + E_WIN]
    cat = jnp.concatenate([p[...] for p in pieces], axis=0)
    _, part, _ = place_of(sz, lax.broadcasted_iota(jnp.int32, (sz.spread, sz.count), 0))
    for q in range(sz.parts):
        columns = slice(q * sz.cols, (q + 1) * sz.cols)
        if weighted:
            mine = jnp.where(part == q, w[...], 0.0)
            high = mine.astype(BF16)
            low = (mine - high.astype(F32)).astype(BF16)
            total = mm(high, cat, 0, 0) + mm(low, cat, 0, 0)
        else:
            total = mm(jnp.where(part == q, w[...].astype(F32), 0.0).astype(BF16), cat, 0, 0)
        out[:, columns] = (values[:, columns].astype(F32) + total).astype(BF16)


def lay_rows(sz, slices, rows):
    me = lax.rem(lax.axis_index("expert"), sz.split)
    for j, s in enumerate(slices):
        at = lax.rem(me + sz.split - j, sz.split) * sz.width
        rows[:, pl.ds(pl.multiple_of(at, 128), sz.width)] = s[...]


def load_kernel(weight, after, held, sems):
    block = weight.shape[0] // sems.shape[0]
    cut = [pl.ds(n * block, block) for n in range(sems.shape[0])]
    for c in fetch([(weight.at[c], held.at[c]) for c in cut], sems):
        c.wait()


def load_and_pre_kernel(sz, chunks, *refs):
    n = sz.split
    slices, (wg, wu, wg_near, wu_near, gate, up, rows, turned, sems) = refs[:n], refs[n:]
    block = sz.hidden // chunks
    cut = [pl.ds(c * block, block) for c in range(chunks)]
    steps = [(src.at[c], dst, c, out) for c in cut for src, dst, out in ((wg, wg_near, gate), (wu, wu_near, up))]
    copies = [pltpu.make_async_copy(src, dst.at[c], sems.at[n]) for n, (src, dst, c, _) in enumerate(steps)]
    ahead = 3
    always = lax.axis_index("expert") >= 0
    for c in copies[:ahead]:
        c.start()
    lay_rows(sz, slices, rows)
    turned[...] = rows[...].T
    for n, (_, dst, c, out) in enumerate(steps):
        copies[n].wait()
        if n + ahead < len(steps):
            copies[n + ahead].start()

        @pl.when(always)
        def _(dst=dst, c=c, out=out):
            out[c, :] = mm(dst[c, :], turned[...])


def columns_of(sz, j):
    me = lax.rem(lax.axis_index("expert"), sz.split)
    at = lax.rem(me + j, sz.split) * sz.width
    block = min(512, sz.width)
    return [
        (pl.ds(n * block, block), pl.ds(pl.multiple_of(at + n * block, 128), block))
        for n in range(sz.width // block)
    ]


def backward_slices(sz, js, d_gate, d_up, wg, wu, outs):
    for j, out in zip(js, outs):
        for here, there in columns_of(sz, j):
            out[:, here] = (mm(d_gate, wg[:, there]) + mm(d_up, wu[:, there])).astype(BF16)


def forward_slices(sz, js, hidden, wd, outs):
    for j, out in zip(js, outs):
        for here, there in columns_of(sz, j):
            out[:, here] = mm(hidden, wd[:, there]).astype(BF16)


def backward_kernel(sz, *refs):
    n = sz.split
    slices, (gate, up, wd, wg, wu, d_gate, d_up), outs, rows = refs[:n], refs[n : n + 7], refs[n + 7 : -1], refs[-1]
    lay_rows(sz, slices, rows)
    dh = mm(wd[...], rows[...].T)
    g = gate[...]
    sig = jax.nn.sigmoid(g)
    d_up[...] = (dh * (g * sig)).T.astype(BF16)
    d_gate[...] = (dh * up[...] * sig * (1.0 + g * (1.0 - sig))).T.astype(BF16)
    backward_slices(sz, range(1, n), d_gate[...], d_up[...], wg, wu, outs)


def backward_own_kernel(sz, d_gate, d_up, wg, wu, out):
    backward_slices(sz, (0,), d_gate[...], d_up[...], wg, wu, (out,))


def forward_kernel(sz, *refs):
    n = sz.split
    slices, (wg, wu, wd, hidden), outs, rows = refs[:n], refs[n : n + 4], refs[n + 4 : -1], refs[-1]
    lay_rows(sz, slices, rows)
    turned = rows[...].T
    gate = mm(wg[...], turned)
    up = mm(wu[...], turned)
    hidden[...] = (gate * jax.nn.sigmoid(gate) * up).T.astype(BF16)
    forward_slices(sz, range(1, n), hidden[...], wd, outs)


def forward_own_kernel(sz, hidden, wd, out):
    forward_slices(sz, (0,), hidden[...], wd, (out,))


def near(kernel, outs, args, name, us=0.3, far=(), scratch=()):
    spec = lambda i: pl.BlockSpec(memory_space=pltpu.HBM if i in far else pltpu.VMEM)
    args = [pltpu.with_memory_space_constraint(a, pltpu.HBM) if i in far else a for i, a in enumerate(args)]
    return pl.pallas_call(
        kernel,
        out_shape=[jax.ShapeDtypeStruct(s, d) for s, d in outs],
        name=name,
        in_specs=[spec(i) for i in range(len(args))],
        out_specs=[pl.BlockSpec(memory_space=pltpu.VMEM) for _ in outs],
        scratch_shapes=list(scratch),
        compiler_params=pltpu.CompilerParams(vmem_limit_bytes=VMEM_LIMIT),
        cost_estimate=pl.CostEstimate(flops=int(us * 1.1e9), bytes_accessed=1 << 16, transcendentals=0),
    )(*args)


def shards(
    section_acts,
    section_input_gradients,
    saved_input,
    fwd_routes,
    fwd_probs,
    back_routes,
    back_probs,
    w_gate,
    w_up,
    w_down,
):
    experts = lax.axis_size("expert")
    sections = lax.axis_size("section")
    split = experts // E_WIN
    acts, grads, saved = section_acts[0], section_input_gradients[0], saved_input[0]
    wg, wu, wd = w_gate[0], w_up[0], w_down[0]
    count, width = acts.shape
    sz = Sizes(count, width, wg.shape[0], split)
    full = width * split
    piece = ((sz.piece, sz.cols), BF16)
    rows = ((sz.slots, width), BF16)

    def by_section(x, by):
        return lax.ppermute(x, "section", [(i, (i + by) % sections) for i in range(sections)])

    def to_expert(x, offset, by):
        pairs = [
            (e * sections + n, ((e // split ^ offset) * split + e % split) * sections + (n + by) % sections)
            for e in range(experts)
            for n in range(sections)
        ]
        return lax.ppermute(x, ("expert", "section"), pairs)

    def exchange(pieces, by=0):
        return [p if o == 0 and by == 0 else to_expert(p, o, by) for o, p in enumerate(pieces)]

    def along_group(x, by):
        pairs = [(e, e // split * split + (e + by) % split) for e in range(experts)]
        return lax.ppermute(x, "expert", pairs)

    def gather(x):
        return [x] + [along_group(x, j) for j in range(1, split)]

    def scatter(slices):
        return [along_group(s, j) for j, s in enumerate(slices, 1)]

    part = functools.partial
    pieces = [piece] * E_WIN
    block = ((count, width), BF16)
    held = ((sz.spread, sz.cols), BF16)
    route_scratch = [pltpu.VMEM(fwd_routes.shape[:0:-1], d) for d in (jnp.int32, F32)]
    block_scratch = pltpu.VMEM((count, width), BF16)
    rows_scratch = pltpu.VMEM((sz.slots, full), BF16)

    fr, fp, br, bp = fwd_routes[0].T, fwd_probs[0].T, back_routes[0].T, back_probs[0].T
    br_next, bp_next = by_section(back_routes, 1)[0].T, by_section(back_probs, 1)[0].T
    fr_next = by_section(fwd_routes, -1)[0].T
    w_f, w_b, *b_out = near(
        part(local_kernel, sz),
        [((sz.spread, count), F32), ((sz.spread, count), BF16)] + pieces,
        (fr, fp, br, bp, saved),
        "local",
        2.0,
        far=range(5),
        scratch=route_scratch * 2 + [block_scratch, pltpu.SemaphoreType.DMA((5,))],
    )
    picked = near(
        part(pick_kernel, sz),
        pieces * 2,
        (br_next, bp_next, fr_next, grads, acts, w_b),
        "pick",
        2.0,
        far=(3, 4),
        scratch=[block_scratch, block_scratch, pltpu.SemaphoreType.DMA((2,))],
    )
    g_in = exchange(picked[:E_WIN], -1)
    x_in = exchange(picked[E_WIN:], 1)
    b_in = exchange(b_out)
    wd_near = near(
        load_kernel, [(wd.shape, BF16)], (wd, picked[0]), "load", 3.5, far=(0,), scratch=[pltpu.SemaphoreType.DMA((2,))]
    )[0]
    unpicked = lambda pieces, name: near(part(unpick_kernel, sz), [rows], pieces, name)[0]
    b_rows = gather(unpicked(b_in, "unpick_saved"))
    g_rows = gather(unpicked(g_in, "unpick_gradients"))
    x_rows = gather(unpicked(x_in, "unpick_acts"))

    chunks = 4
    hidden_f32 = ((sz.hidden, sz.slots), F32)
    hidden_bf16 = ((sz.slots, sz.hidden), BF16)
    wg_near, wu_near, gate, up = near(
        part(load_and_pre_kernel, sz, chunks),
        [(wg.shape, BF16)] * 2 + [hidden_f32] * 2,
        (*b_rows, wg, wu),
        "pre",
        6.0,
        far=(split, split + 1),
        scratch=[rows_scratch, pltpu.VMEM((full, sz.slots), BF16), pltpu.SemaphoreType.DMA((2 * chunks,))],
    )
    d_gate, d_up, *back = near(
        part(backward_kernel, sz),
        [hidden_bf16] * 2 + [rows] * (split - 1),
        (*g_rows, gate, up, wd_near, wg_near, wu_near),
        "backward",
        4.0,
        scratch=[rows_scratch],
    )
    back_in = scatter(back)
    back_own = near(part(backward_own_kernel, sz), [rows], (d_gate, d_up, wg_near, wu_near), "backward_own", 2.0)
    hidden, *made = near(
        part(forward_kernel, sz),
        [hidden_bf16] + [rows] * (split - 1),
        (*x_rows, wg_near, wu_near, wd_near),
        "forward",
        5.0,
        scratch=[rows_scratch],
    )
    made_in = scatter(made)
    made_own = near(part(forward_own_kernel, sz), [rows], (hidden, wd_near), "forward_own", 1.0)
    back_pieces = exchange(near(part(fold_kernel, sz), pieces, (*back_own, *back_in), "fold_backward"))
    made_pieces = exchange(near(part(fold_kernel, sz), pieces, (*made_own, *made_in), "fold_forward"))

    acts, grads, *_ = lax.optimization_barrier((acts, grads, *g_in, *x_in))
    x_full, dy_full = by_section(acts, 1), by_section(grads, -1)
    input_grads = near(part(combine_kernel, sz, False), [block], (dy_full, w_b, *back_pieces), "combine_gradients", 1.5)[0]
    section_out = near(part(combine_kernel, sz, True), [block], (x_full, w_f, *made_pieces), "combine_acts", 1.5)[0]
    return (section_out[None], input_grads[None])


def solution(mesh):
    return jax.shard_map(
        shards,
        mesh=mesh,
        in_specs=(
            P("section", "expert", None),
            P("section", "expert", None),
            P("section", "expert", None),
            P("section", None, None),
            P("section", None, None),
            P("section", None, None),
            P("section", None, None),
            P("section", "expert", None),
            P("section", "expert", None),
            P("section", "expert", None),
        ),
        out_specs=(P("section", "expert", None), P("section", "expert", None)),
        check_vma=False,
    )
```

```python
import functools
import jax
import jax.numpy as jnp
from jax import lax
from jax.experimental import pallas as pl
from jax.experimental.pallas import tpu as pltpu
from jax.sharding import PartitionSpec as P

N_ROUTED = 256
TOP = 8
E_WIN = 4
F32 = jnp.float32
BF16 = jnp.bfloat16
VMEM_LIMIT = 8 << 20


def mm(a, b, ca=1, cb=0, precision=None):
    dims = (((ca,), (cb,)), ((), ()))
    return lax.dot_general(a, b, dims, precision=precision, preferred_element_type=F32)


class Sizes:
    def __init__(self, count, width, hidden, split):
        self.count, self.width, self.hidden, self.split = count, width, hidden, split
        self.cap = count * TOP * 2 // N_ROUTED
        self.slots = E_WIN * self.cap
        self.parts = min(4, width // 128)
        self.cols = width // self.parts
        self.piece = self.parts * self.cap
        self.spread = E_WIN * self.piece


def place_of(sz, i):
    piece = sum([(i >= sz.piece * n).astype(jnp.int32) for n in range(1, E_WIN)])
    i = i - sz.piece * piece
    part = sum([(i >= sz.cap * n).astype(jnp.int32) for n in range(1, sz.parts)])
    return piece, part, i - sz.cap * part


def one_hot(mask):
    return jnp.where(mask, 1.0, 0.0).astype(BF16)


def route_masks(routes, probs, expert, place, earlier):
    chosen = jnp.zeros(expert.shape, F32)
    weight = jnp.zeros(expert.shape, F32)
    for c in range(TOP):
        hit = routes[c : c + 1, :] == expert
        chosen += jnp.where(hit, 1.0, 0.0)
        if probs is not None:
            weight += jnp.where(hit, probs[c : c + 1, :], 0.0)
    before = mm(chosen.astype(BF16), earlier)
    mask = (chosen > 0.5) & (jnp.abs(before - place.astype(F32)) < 0.5)
    return mask, weight


def my_group(ref, group, count):
    block = ref[:, :count]
    for n in range(1, E_WIN):
        block = jnp.where(group == n, ref[:, n * count : (n + 1) * count], block)
    return block


def earlier_tokens(sz):
    shape = (sz.count, sz.count)
    return one_hot(lax.broadcasted_iota(jnp.int32, shape, 0) < lax.broadcasted_iota(jnp.int32, shape, 1))


def piece_masks(sz, routes_ref, probs_ref):
    group = lax.axis_index("expert") // sz.split
    shape = (sz.spread, sz.count)
    piece, part, place = place_of(sz, lax.broadcasted_iota(jnp.int32, shape, 0))
    routes = my_group(routes_ref, group, sz.count)
    probs = None if probs_ref is None else my_group(probs_ref, group, sz.count)
    mask, weight = route_masks(routes, probs, piece ^ group, place, earlier_tokens(sz))
    return mask, weight, part


def pick(sz, mask, part, values):
    picked = jnp.zeros((sz.spread, sz.cols), F32)
    for q in range(sz.parts):
        picked += mm(one_hot(mask & (part == q)), values[:, q * sz.cols : (q + 1) * sz.cols])
    return picked


def put_pieces(values, outs):
    step = values.shape[0] // len(outs)
    for n, out in enumerate(outs):
        out[...] = values[n * step : (n + 1) * step].astype(BF16)


def fetch(pairs, sems):
    copies = [pltpu.make_async_copy(src, dst, sems.at[n]) for n, (src, dst) in enumerate(pairs)]
    for c in copies:
        c.start()
    return copies


def local_kernel(sz, fr, fp, br, bp, saved, w_f, m_f, m_b, scale, *rest):
    pieces, (fr_v, fp_v, br_v, bp_v, saved_v, sems) = rest[:E_WIN], rest[E_WIN:]
    pairs = [(br, br_v), (bp, bp_v), (fr, fr_v), (fp, fp_v), (saved, saved_v)]
    copies = fetch(pairs, sems)
    for c in copies[:4]:
        c.wait()
    mask, weight, part = piece_masks(sz, br_v, bp_v)
    m_b[...] = one_hot(mask)
    total = jnp.sum(jnp.where(mask, weight, 0.0), axis=1, keepdims=True)
    scale[...] = jnp.broadcast_to(total, scale.shape)
    copies[4].wait()
    put_pieces(pick(sz, mask, part, saved_v), pieces)
    mask, weight, _ = piece_masks(sz, fr_v, fp_v)
    m_f[...] = one_hot(mask)
    w_f[...] = jnp.where(mask, weight, 0.0)


def pick_again_kernel(sz, scaled, chosen, *refs):
    values, pieces = refs[scaled], refs[scaled + 1 :]
    _, part, _ = place_of(sz, lax.broadcasted_iota(jnp.int32, (sz.spread, sz.count), 0))
    picked = pick(sz, chosen[...].astype(F32) > 0.5, part, values)
    put_pieces(picked * refs[0][:, 0:1] if scaled else picked, pieces)


def end_to_end(pieces):
    return jnp.concatenate([p[...] for p in (pieces[0], *pieces[:0:-1])], axis=0)


def unpick(sz, cat, rows):
    shape = (sz.slots, sz.spread)
    slot = lax.broadcasted_iota(jnp.int32, shape, 0)
    piece, part, place = place_of(sz, lax.broadcasted_iota(jnp.int32, shape, 1))
    here = slot == piece * sz.cap + place
    for q in range(sz.parts):
        rows[:, q * sz.cols : (q + 1) * sz.cols] = mm(one_hot(here & (part == q)), cat).astype(BF16)


def unpick_kernel(sz, *refs):
    unpick(sz, end_to_end(refs[:-1]), refs[-1])


def fold_kernel(sz, *refs):
    slices, pieces = refs[: sz.split], refs[sz.split :]
    rows = slices[0][...].astype(F32)
    for s in slices[1:]:
        rows += s[...].astype(F32)
    rows = rows.astype(BF16)
    shape = (sz.spread, sz.slots)
    piece, part, place = place_of(sz, lax.broadcasted_iota(jnp.int32, shape, 0))
    here = lax.broadcasted_iota(jnp.int32, shape, 1) == piece * sz.cap + place
    out = jnp.zeros((sz.spread, sz.cols), F32)
    for q in range(sz.parts):
        out += mm(one_hot(here & (part == q)), rows[:, q * sz.cols : (q + 1) * sz.cols])
    put_pieces(out, pieces)


def combine_kernel(sz, copies, values, w, *refs):
    pieces, (out, done, sems) = refs[:E_WIN], refs[E_WIN:]
    cat = end_to_end(pieces)
    stores = []
    for q in range(sz.parts):
        columns = pl.ds(q * sz.cols, sz.cols)
        total = values[:, columns].astype(F32)
        for n in range(copies):
            total += mm(w[q * copies + n], cat)
        done[:, columns] = total.astype(BF16)
        stores.append(pltpu.make_async_copy(done.at[:, columns], out.at[:, columns], sems.at[q]))
        stores[-1].start()
    for store in stores:
        store.wait()


def lay_rows(sz, slices, rows):
    me = lax.rem(lax.axis_index("expert"), sz.split)
    for j, s in enumerate(slices):
        at = lax.rem(me + sz.split - j, sz.split) * sz.width
        rows[:, pl.ds(pl.multiple_of(at, 128), sz.width)] = s[...]


def load_kernel(sz, w_f, w_b, wg, wu, wg_near, wu_near, f_turned, b_turned, sems):
    copies = fetch([(wg, wg_near), (wu.at[: wu_near.shape[0]], wu_near)], sems)
    _, part, _ = place_of(sz, lax.broadcasted_iota(jnp.int32, (sz.count, sz.spread), 1))
    f = w_f[...].T
    b = w_b[...].astype(F32).T
    for q in range(sz.parts):
        mine = jnp.where(part == q, f, 0.0)
        high = mine.astype(BF16)
        f_turned[2 * q] = high
        f_turned[2 * q + 1] = (mine - high.astype(F32)).astype(BF16)
        b_turned[q] = jnp.where(part == q, b, 0.0).astype(BF16)
    for c in copies:
        c.wait()


def load_one_kernel(weight, held, sems):
    half = weight.shape[0] // 2
    for c in fetch([(weight.at[cut], held.at[cut]) for cut in (pl.ds(0, half), pl.ds(half, half))], sems):
        c.wait()


def by_halves(weight, turned, out):
    half = weight.shape[0] // 2
    for cut in (slice(0, half), slice(half, None)):
        out[cut, :] = mm(weight[cut, :], turned[...])


def first_kernel(sz, *refs):
    n, m, half = sz.split, sz.slots, sz.hidden // 2
    b_slices, x_slices, (wg, wu_0, wu, wd), refs = refs[:n], refs[n : 2 * n], refs[2 * n : 2 * n + 4], refs[2 * n + 4 :]
    wu_1, gate, up, hidden, *outs = refs[:-5]
    rows, turned, gate_all, up_all, sems = refs[-5:]
    (copy,) = fetch([(wu.at[half:], wu_1)], sems)
    lay_rows(sz, b_slices, rows)
    turned[:, :m] = rows[...].T
    lay_rows(sz, x_slices, rows)
    turned[:, m:] = rows[...].T
    by_halves(wg, turned, gate_all)
    up_all[:half, :] = mm(wu_0[...], turned[...])

    @pl.when(lax.axis_index("expert") >= 0)
    def _():
        copy.wait()
        up_all[half:, :] = mm(wu_1[...], turned[...])

    g = gate_all[:, m:]
    hidden[...] = (g * jax.nn.sigmoid(g) * up_all[:, m:]).T.astype(BF16)
    gate[...] = gate_all[:, :m]
    up[...] = up_all[:, :m]
    forward_slices(sz, range(1, n), hidden, wd, outs)


def columns_of(sz, j):
    me = lax.rem(lax.axis_index("expert"), sz.split)
    at = lax.rem(me + j, sz.split) * sz.width
    block = min(512, sz.width)
    return [
        (pl.ds(n * block, block), pl.ds(pl.multiple_of(at + n * block, 128), block))
        for n in range(sz.width // block)
    ]


def backward_slices(sz, js, d_gate, d_up, wg, wu_0, wu_1, outs):
    half = wu_0.shape[0]
    for j, out in zip(js, outs):
        for here, there in columns_of(sz, j):
            total = mm(d_gate[...], wg[:, there]) + mm(d_up[:, :half], wu_0[:, there]) + mm(d_up[:, half:], wu_1[:, there])
            out[:, here] = total.astype(BF16)


def forward_slices(sz, js, hidden, wd, outs):
    for j, out in zip(js, outs):
        for here, there in columns_of(sz, j):
            out[:, here] = mm(hidden[...], wd[:, there]).astype(BF16)


def backward_kernel(sz, *refs):
    n = sz.split
    slices, (gate, up, wg, wu_0, wu_1, wd), refs = refs[:n], refs[n : n + 6], refs[n + 6 :]
    d_gate, d_up, *outs = refs[:-3]
    rows, turned, dh = refs[-3:]
    lay_rows(sz, slices, rows)
    turned[...] = rows[...].T
    by_halves(wd, turned, dh)
    dh = dh[...]
    g = gate[...]
    sig = jax.nn.sigmoid(g)
    d_up[...] = (dh * (g * sig)).T.astype(BF16)
    d_gate[...] = (dh * up[...] * sig * (1.0 + g * (1.0 - sig))).T.astype(BF16)
    backward_slices(sz, range(1, n), d_gate, d_up, wg, wu_0, wu_1, outs)


def backward_own_kernel(sz, d_gate, d_up, wg, wu_0, wu_1, out):
    backward_slices(sz, (0,), d_gate, d_up, wg, wu_0, wu_1, (out,))


def forward_own_kernel(sz, hidden, wd, out):
    forward_slices(sz, (0,), hidden, wd, (out,))


def near(kernel, outs, args, name, us=0.3, far=(), scratch=(), after=(), far_outs=False):
    spaces = [pltpu.HBM if i in far else pltpu.VMEM for i in range(len(args))] + [pl.ANY] * len(after)
    args = [pltpu.with_memory_space_constraint(a, pltpu.HBM) if i in far else a for i, a in enumerate(args)]

    def body(*refs):
        kernel(*refs[: len(args)], *refs[len(args) + len(after) :])

    return pl.pallas_call(
        body,
        out_shape=[jax.ShapeDtypeStruct(s, d) for s, d in outs],
        name=name,
        in_specs=[pl.BlockSpec(memory_space=s) for s in spaces],
        out_specs=[pl.BlockSpec(memory_space=pltpu.HBM if far_outs else pltpu.VMEM) for _ in outs],
        scratch_shapes=list(scratch),
        compiler_params=pltpu.CompilerParams(vmem_limit_bytes=VMEM_LIMIT),
        cost_estimate=pl.CostEstimate(flops=int(us * 1.1e9), bytes_accessed=1 << 16, transcendentals=0),
    )(*args, *after)


def shards(
    section_acts,
    section_input_gradients,
    saved_input,
    fwd_routes,
    fwd_probs,
    back_routes,
    back_probs,
    w_gate,
    w_up,
    w_down,
):
    experts = lax.axis_size("expert")
    sections = lax.axis_size("section")
    split = experts // E_WIN
    acts, grads, saved = section_acts[0], section_input_gradients[0], saved_input[0]
    wg, wu, wd = w_gate[0], w_up[0], w_down[0]
    count, width = acts.shape
    sz = Sizes(count, width, wg.shape[0], split)
    full = width * split
    piece = ((sz.piece, sz.cols), BF16)
    rows = ((sz.slots, width), BF16)

    def by_section(x, by):
        return lax.ppermute(x, "section", [(i, (i + by) % sections) for i in range(sections)])

    def exchange(pieces):
        pairs = lambda o: [(e, (e // split ^ o) * split + e % split) for e in range(experts)]
        return [pieces[0]] + [lax.ppermute(pieces[o], "expert", pairs(o)) for o in range(E_WIN - 1, 0, -1)]

    def along_group(x, by):
        pairs = [(e, e // split * split + (e + by) % split) for e in range(experts)]
        return lax.ppermute(x, "expert", pairs)

    def gather(x):
        return [x] + [along_group(x, j) for j in range(1, split)]

    def scatter(slices):
        return tuple(along_group(s, j) for j, s in enumerate(slices, 1))

    part = functools.partial
    pieces = [piece] * E_WIN
    block = ((count, width), BF16)
    held = ((sz.spread, sz.cols), BF16)
    route_scratch = [pltpu.VMEM(fwd_routes.shape[:0:-1], d) for d in (jnp.int32, F32)]
    block_scratch = pltpu.VMEM((count, width), BF16)
    rows_scratch = pltpu.VMEM((sz.slots, full), BF16)

    fr, fp, br, bp = fwd_routes[0].T, fwd_probs[0].T, back_routes[0].T, back_probs[0].T
    x_full = by_section(acts, 1)
    half_weight = ((sz.hidden // 2, full), BF16)
    table = (sz.spread, count)
    w_f, m_f, m_b, scale, *b_out = near(
        part(local_kernel, sz),
        [(table, F32), (table, BF16), (table, BF16), ((sz.spread, 128), F32)] + pieces,
        (fr, fp, br, bp, saved),
        "local",
        2.0,
        far=range(5),
        scratch=route_scratch * 2 + [block_scratch, pltpu.SemaphoreType.DMA((5,))],
    )
    b_in = exchange(b_out)
    grads, m_b = lax.optimization_barrier((grads, m_b))
    dy_full = by_section(grads, -1)
    wg_near, wu_0, f_turned, b_turned = near(
        part(load_kernel, sz),
        [(wg.shape, BF16), half_weight] + [((n * sz.parts, count, sz.spread), BF16) for n in (2, 1)],
        (w_f, m_b, wg, wu),
        "load",
        4.0,
        far=(2, 3),
        scratch=[pltpu.SemaphoreType.DMA((2,))],
    )
    unpicked = lambda pieces, name, after=(): near(part(unpick_kernel, sz), [rows], pieces, name, after=after)[0]
    b_near = unpicked(b_in, "unpick_saved", (f_turned,))
    x_out = near(part(pick_again_kernel, sz, 0), pieces, (m_f, x_full), "pick_acts", 0.5, after=(b_near,))
    x_in = exchange(x_out)
    g_out = near(
        part(pick_again_kernel, sz, 1), pieces, (m_b, scale, dy_full), "pick_gradients", 0.5, after=x_out[:1]
    )
    x_near = unpicked(x_in, "unpick_acts", g_out[:1])
    wd_near = near(
        load_one_kernel, [(wd.shape, BF16)], (wd,), "load_down", 3.0, far=(0,), scratch=[pltpu.SemaphoreType.DMA((2,))], after=(x_near,)
    )[0]
    g_in = exchange(g_out)
    g_near = unpicked(g_in, "unpick_gradients", (wd_near,))
    b_rows, x_rows, g_rows = gather(b_near), gather(x_near), gather(g_near)

    hidden_f32 = ((sz.hidden, sz.slots), F32)
    hidden_bf16 = ((sz.slots, sz.hidden), BF16)
    both = pltpu.VMEM((sz.hidden, 2 * sz.slots), F32)
    wu_1, gate, up, hidden, *made = near(
        part(first_kernel, sz),
        [half_weight] + [hidden_f32] * 2 + [hidden_bf16] + [rows] * (split - 1),
        (*b_rows, *x_rows, wg_near, wu_0, wu, wd_near),
        "first",
        6.0,
        far=(2 * split + 2,),
        scratch=[rows_scratch, pltpu.VMEM((full, 2 * sz.slots), BF16), both, both, pltpu.SemaphoreType.DMA((1,))],
        after=(g_near,),
    )
    made_in = scatter(made)
    up_weights = (wg_near, wu_0, wu_1)
    d_gate, d_up, *back = near(
        part(backward_kernel, sz),
        [hidden_bf16] * 2 + [rows] * (split - 1),
        (*g_rows, gate, up, *up_weights, wd_near),
        "backward",
        4.0,
        scratch=[rows_scratch, pltpu.VMEM((full, sz.slots), BF16), pltpu.VMEM((sz.hidden, sz.slots), F32)],
    )
    back_in = scatter(back)
    made_own = near(part(forward_own_kernel, sz), [rows], (hidden, wd_near), "forward_own", 1.0, after=(d_gate,))
    made_pieces = near(part(fold_kernel, sz), pieces, (*made_own, *made_in), "fold_forward")
    back_own = near(
        part(backward_own_kernel, sz), [rows], (d_gate, d_up, *up_weights), "backward_own", 1.5, after=made_pieces[:1]
    )
    made_pieces = exchange(made_pieces)
    back_pieces = exchange(near(part(fold_kernel, sz), pieces, (*back_own, *back_in), "fold_backward"))

    combine = lambda copies, args, name, after: near(
        part(combine_kernel, sz, copies),
        [block],
        args,
        name,
        1.2,
        scratch=[block_scratch, pltpu.SemaphoreType.DMA((sz.parts,))],
        after=after,
        far_outs=True,
    )[0]
    section_out = combine(2, (x_full, f_turned, *made_pieces), "combine_acts", back_pieces[:1])
    input_grads = combine(1, (dy_full, b_turned, *back_pieces), "combine_gradients", ())
    return (section_out[None], input_grads[None])


def solution(mesh):
    return jax.shard_map(
        shards,
        mesh=mesh,
        in_specs=(
            P("section", "expert", None),
            P("section", "expert", None),
            P("section", "expert", None),
            P("section", None, None),
            P("section", None, None),
            P("section", None, None),
            P("section", None, None),
            P("section", "expert", None),
            P("section", "expert", None),
            P("section", "expert", None),
        ),
        out_specs=(P("section", "expert", None), P("section", "expert", None)),
        check_vma=False,
    )
```

```python
import functools
import jax
import jax.numpy as jnp
from jax import lax
from jax.experimental import pallas as pl
from jax.experimental.pallas import tpu as pltpu
from jax.sharding import PartitionSpec as P

N_ROUTED = 256
TOP = 8
E_WIN = 4
F32 = jnp.float32
BF16 = jnp.bfloat16
VMEM_LIMIT = 8 << 20


def mm(a, b, ca=1, cb=0, precision=None):
    dims = (((ca,), (cb,)), ((), ()))
    return lax.dot_general(a, b, dims, precision=precision, preferred_element_type=F32)


class Sizes:
    def __init__(self, count, width, hidden, split):
        self.count, self.width, self.hidden, self.split = count, width, hidden, split
        self.cap = count * TOP * 2 // N_ROUTED
        self.slots = E_WIN * self.cap
        self.parts = min(4, width // 128)
        self.cols = width // self.parts
        self.piece = self.parts * self.cap
        self.spread = E_WIN * self.piece


def place_of(sz, i):
    piece = sum([(i >= sz.piece * n).astype(jnp.int32) for n in range(1, E_WIN)])
    i = i - sz.piece * piece
    part = sum([(i >= sz.cap * n).astype(jnp.int32) for n in range(1, sz.parts)])
    return piece, part, i - sz.cap * part


def one_hot(mask):
    return jnp.where(mask, 1.0, 0.0).astype(BF16)


def route_masks(routes, probs, expert, place, earlier):
    chosen = jnp.zeros(expert.shape, F32)
    weight = jnp.zeros(expert.shape, F32)
    for c in range(TOP):
        hit = routes[c : c + 1, :] == expert
        chosen += jnp.where(hit, 1.0, 0.0)
        if probs is not None:
            weight += jnp.where(hit, probs[c : c + 1, :], 0.0)
    before = mm(chosen.astype(BF16), earlier)
    mask = (chosen > 0.5) & (jnp.abs(before - place.astype(F32)) < 0.5)
    return mask, weight


def my_group(ref, group, count):
    block = ref[:, :count]
    for n in range(1, E_WIN):
        block = jnp.where(group == n, ref[:, n * count : (n + 1) * count], block)
    return block


def earlier_tokens(sz):
    shape = (sz.count, sz.count)
    return one_hot(lax.broadcasted_iota(jnp.int32, shape, 0) < lax.broadcasted_iota(jnp.int32, shape, 1))


def piece_masks(sz, routes_ref, probs_ref):
    group = lax.axis_index("expert") // sz.split
    shape = (sz.spread, sz.count)
    piece, part, place = place_of(sz, lax.broadcasted_iota(jnp.int32, shape, 0))
    routes = my_group(routes_ref, group, sz.count)
    probs = None if probs_ref is None else my_group(probs_ref, group, sz.count)
    mask, weight = route_masks(routes, probs, piece ^ group, place, earlier_tokens(sz))
    return mask, weight, part


def pick(sz, mask, part, values):
    picked = jnp.zeros((sz.spread, sz.cols), F32)
    for q in range(sz.parts):
        picked += mm(one_hot(mask & (part == q)), values[:, q * sz.cols : (q + 1) * sz.cols])
    return picked


def put_pieces(values, outs):
    step = values.shape[0] // len(outs)
    for n, out in enumerate(outs):
        out[...] = values[n * step : (n + 1) * step].astype(BF16)


def fetch(pairs, sems):
    copies = [pltpu.make_async_copy(src, dst, sems.at[n]) for n, (src, dst) in enumerate(pairs)]
    for c in copies:
        c.start()
    return copies


def local_kernel(sz, fr, fp, br, bp, saved, w_f, m_f, m_b, scale, *rest):
    pieces, (fr_v, fp_v, br_v, bp_v, saved_v, sems) = rest[:E_WIN], rest[E_WIN:]
    pairs = [(br, br_v), (bp, bp_v), (fr, fr_v), (fp, fp_v), (saved, saved_v)]
    copies = fetch(pairs, sems)
    for c in copies[:4]:
        c.wait()
    mask, weight, part = piece_masks(sz, br_v, bp_v)
    m_b[...] = one_hot(mask)
    total = jnp.sum(jnp.where(mask, weight, 0.0), axis=1, keepdims=True)
    scale[...] = jnp.broadcast_to(total, scale.shape)
    copies[4].wait()
    put_pieces(pick(sz, mask, part, saved_v), pieces)
    mask, weight, _ = piece_masks(sz, fr_v, fp_v)
    m_f[...] = one_hot(mask)
    w_f[...] = jnp.where(mask, weight, 0.0)


def pick_again_kernel(sz, scaled, chosen, *refs):
    values, pieces = refs[scaled], refs[scaled + 1 :]
    _, part, _ = place_of(sz, lax.broadcasted_iota(jnp.int32, (sz.spread, sz.count), 0))
    picked = pick(sz, chosen[...].astype(F32) > 0.5, part, values)
    put_pieces(picked * refs[0][:, 0:1] if scaled else picked, pieces)


def end_to_end(pieces):
    return jnp.concatenate([p[...] for p in (pieces[0], *pieces[:0:-1])], axis=0)


def unpick(sz, cat, rows):
    shape = (sz.slots, sz.spread)
    slot = lax.broadcasted_iota(jnp.int32, shape, 0)
    piece, part, place = place_of(sz, lax.broadcasted_iota(jnp.int32, shape, 1))
    here = slot == piece * sz.cap + place
    for q in range(sz.parts):
        rows[:, q * sz.cols : (q + 1) * sz.cols] = mm(one_hot(here & (part == q)), cat).astype(BF16)


def unpick_kernel(sz, *refs):
    unpick(sz, end_to_end(refs[:-1]), refs[-1])


def fold_kernel(sz, *refs):
    slices, pieces = refs[: sz.split], refs[sz.split :]
    rows = slices[0][...].astype(F32)
    for s in slices[1:]:
        rows += s[...].astype(F32)
    rows = rows.astype(BF16)
    shape = (sz.spread, sz.slots)
    piece, part, place = place_of(sz, lax.broadcasted_iota(jnp.int32, shape, 0))
    here = lax.broadcasted_iota(jnp.int32, shape, 1) == piece * sz.cap + place
    out = jnp.zeros((sz.spread, sz.cols), F32)
    for q in range(sz.parts):
        out += mm(one_hot(here & (part == q)), rows[:, q * sz.cols : (q + 1) * sz.cols])
    put_pieces(out, pieces)


def combine_kernel(sz, copies, values, w, *refs):
    pieces, (out, done, sems) = refs[:E_WIN], refs[E_WIN:]
    cat = end_to_end(pieces)
    stores = []
    for q in range(sz.parts):
        columns = pl.ds(q * sz.cols, sz.cols)
        total = values[:, columns].astype(F32)
        for n in range(copies):
            total += mm(w[q * copies + n], cat)
        done[:, columns] = total.astype(BF16)
        stores.append(pltpu.make_async_copy(done.at[:, columns], out.at[:, columns], sems.at[q]))
        stores[-1].start()
    for store in stores:
        store.wait()


def turn_kernel(sz, w_f, w_b, f_turned, b_turned):
    _, part, _ = place_of(sz, lax.broadcasted_iota(jnp.int32, (sz.count, sz.spread), 1))
    f = w_f[...].T
    b = w_b[...].astype(F32).T
    for q in range(sz.parts):
        mine = jnp.where(part == q, f, 0.0)
        high = mine.astype(BF16)
        f_turned[2 * q] = high
        f_turned[2 * q + 1] = (mine - high.astype(F32)).astype(BF16)
        b_turned[q] = jnp.where(part == q, b, 0.0).astype(BF16)


def add_product(sz, weight, behind, turned, before, out):
    at = lax.rem(lax.axis_index("expert") + sz.split - behind, sz.split) * sz.width
    columns = pl.ds(pl.multiple_of(at, 128), sz.width)
    half = weight.shape[0] // 2
    for cut in (slice(0, half), slice(half, None)):
        product = mm(weight[cut, columns], turned[...])
        out[cut, :] = product if before is None else before[cut, :] + product


def first_own_kernel(sz, b, x, wg, wu, gate_all, up_all, turned):
    turned[:, : sz.slots] = b[...].T
    turned[:, sz.slots :] = x[...].T
    add_product(sz, wg, 0, turned, None, gate_all)
    add_product(sz, wu, 0, turned, None, up_all)


def first_kernel(sz, *refs):
    n, m = sz.split - 1, sz.slots
    b_slices, x_slices, (gate_own, up_own, wg, wu, wd), refs = refs[:n], refs[n : 2 * n], refs[2 * n : 2 * n + 5], refs[2 * n + 5 :]
    gate, up, hidden, *outs = refs[:-3]
    turned, gate_all, up_all = refs[-3:]
    for j, (b, x) in enumerate(zip(b_slices, x_slices)):
        turned[:, :m] = b[...].T
        turned[:, m:] = x[...].T
        add_product(sz, wg, j + 1, turned, gate_own if j == 0 else gate_all, gate_all)
        add_product(sz, wu, j + 1, turned, up_own if j == 0 else up_all, up_all)
    g = gate_all[:, m:]
    hidden[...] = (g * jax.nn.sigmoid(g) * up_all[:, m:]).T.astype(BF16)
    gate[...] = gate_all[:, :m]
    up[...] = up_all[:, :m]
    forward_slices(sz, range(1, sz.split), hidden, wd, outs)


def columns_of(sz, j):
    me = lax.rem(lax.axis_index("expert"), sz.split)
    at = lax.rem(me + j, sz.split) * sz.width
    block = min(512, sz.width)
    return [
        (pl.ds(n * block, block), pl.ds(pl.multiple_of(at + n * block, 128), block))
        for n in range(sz.width // block)
    ]


def backward_slices(sz, js, d_gate, d_up, wg, wu, outs):
    for j, out in zip(js, outs):
        for here, there in columns_of(sz, j):
            out[:, here] = (mm(d_gate[...], wg[:, there]) + mm(d_up[...], wu[:, there])).astype(BF16)


def forward_slices(sz, js, hidden, wd, outs):
    for j, out in zip(js, outs):
        for here, there in columns_of(sz, j):
            out[:, here] = mm(hidden[...], wd[:, there]).astype(BF16)


def hidden_gradient_own_kernel(sz, g, wd, dh, turned):
    turned[...] = g[...].T
    add_product(sz, wd, 0, turned, None, dh)


def backward_kernel(sz, *refs):
    n = sz.split - 1
    slices, (dh_own, gate, up, wg, wu, wd), refs = refs[:n], refs[n : n + 6], refs[n + 6 :]
    d_gate, d_up, *outs = refs[:-2]
    turned, dh_all = refs[-2:]
    for j, s in enumerate(slices):
        turned[...] = s[...].T
        add_product(sz, wd, j + 1, turned, dh_own if j == 0 else dh_all, dh_all)
    dh = dh_all[...]
    g = gate[...]
    sig = jax.nn.sigmoid(g)
    d_up[...] = (dh * (g * sig)).T.astype(BF16)
    d_gate[...] = (dh * up[...] * sig * (1.0 + g * (1.0 - sig))).T.astype(BF16)
    backward_slices(sz, range(1, sz.split), d_gate, d_up, wg, wu, outs)


def backward_own_kernel(sz, d_gate, d_up, wg, wu, out):
    backward_slices(sz, (0,), d_gate, d_up, wg, wu, (out,))


def forward_own_kernel(sz, hidden, wd, out):
    forward_slices(sz, (0,), hidden, wd, (out,))


def near(kernel, outs, args, name, us=0.3, far=(), scratch=(), after=(), far_outs=False):
    spaces = [pltpu.HBM if i in far else pltpu.VMEM for i in range(len(args))] + [pl.ANY] * len(after)
    args = [pltpu.with_memory_space_constraint(a, pltpu.HBM) if i in far else a for i, a in enumerate(args)]

    def body(*refs):
        kernel(*refs[: len(args)], *refs[len(args) + len(after) :])

    return pl.pallas_call(
        body,
        out_shape=[jax.ShapeDtypeStruct(s, d) for s, d in outs],
        name=name,
        in_specs=[pl.BlockSpec(memory_space=s) for s in spaces],
        out_specs=[pl.BlockSpec(memory_space=pltpu.HBM if far_outs else pltpu.VMEM) for _ in outs],
        scratch_shapes=list(scratch),
        compiler_params=pltpu.CompilerParams(vmem_limit_bytes=VMEM_LIMIT),
        cost_estimate=pl.CostEstimate(flops=int(us * 1.1e9), bytes_accessed=1 << 16, transcendentals=0),
    )(*args, *after)


def shards(
    section_acts,
    section_input_gradients,
    saved_input,
    fwd_routes,
    fwd_probs,
    back_routes,
    back_probs,
    w_gate,
    w_up,
    w_down,
):
    experts = lax.axis_size("expert")
    sections = lax.axis_size("section")
    split = experts // E_WIN
    acts, grads, saved = section_acts[0], section_input_gradients[0], saved_input[0]
    wg, wu, wd = w_gate[0], w_up[0], w_down[0]
    count, width = acts.shape
    sz = Sizes(count, width, wg.shape[0], split)
    full = width * split
    piece = ((sz.piece, sz.cols), BF16)
    rows = ((sz.slots, width), BF16)

    def by_section(x, by):
        return lax.ppermute(x, "section", [(i, (i + by) % sections) for i in range(sections)])

    def exchange(pieces):
        pairs = lambda o: [(e, (e // split ^ o) * split + e % split) for e in range(experts)]
        return [pieces[0]] + [lax.ppermute(pieces[o], "expert", pairs(o)) for o in range(E_WIN - 1, 0, -1)]

    def along_group(x, by):
        pairs = [(e, e // split * split + (e + by) % split) for e in range(experts)]
        return lax.ppermute(x, "expert", pairs)

    def gather(x):
        return [x] + [along_group(x, j) for j in range(1, split)]

    def scatter(slices):
        return tuple(along_group(s, j) for j, s in enumerate(slices, 1))

    part = functools.partial
    pieces = [piece] * E_WIN
    block = ((count, width), BF16)
    held = ((sz.spread, sz.cols), BF16)
    route_scratch = [pltpu.VMEM(fwd_routes.shape[:0:-1], d) for d in (jnp.int32, F32)]
    block_scratch = pltpu.VMEM((count, width), BF16)

    fr, fp, br, bp = fwd_routes[0].T, fwd_probs[0].T, back_routes[0].T, back_probs[0].T
    x_full = by_section(acts, 1)
    table = (sz.spread, count)
    w_f, m_f, m_b, scale, *b_out = near(
        part(local_kernel, sz),
        [(table, F32), (table, BF16), (table, BF16), ((sz.spread, 128), F32)] + pieces,
        (fr, fp, br, bp, saved),
        "local",
        2.0,
        far=range(5),
        scratch=route_scratch * 2 + [block_scratch, pltpu.SemaphoreType.DMA((5,))],
    )
    b_in = exchange(b_out)
    grads, m_b = lax.optimization_barrier((grads, m_b))
    dy_full = by_section(grads, -1)
    f_turned, b_turned = near(
        part(turn_kernel, sz), [((n * sz.parts, count, sz.spread), BF16) for n in (2, 1)], (w_f, m_b), "turn", 4.0
    )
    unpicked = lambda pieces, name, after=(): near(part(unpick_kernel, sz), [rows], pieces, name, after=after)[0]
    b_near = unpicked(b_in, "unpick_saved", (f_turned,))
    x_out = near(part(pick_again_kernel, sz, 0), pieces, (m_f, x_full), "pick_acts", 4.5, after=(b_near,))
    x_in = exchange(x_out)
    g_out = near(
        part(pick_again_kernel, sz, 1), pieces, (m_b, scale, dy_full), "pick_gradients", 0.5, after=x_out[:1]
    )
    x_near = unpicked(x_in, "unpick_acts", g_out[:1])
    both = (sz.hidden, 2 * sz.slots)
    gate_own, up_own = near(
        part(first_own_kernel, sz),
        [(both, F32)] * 2,
        (b_near, x_near, wg, wu),
        "first_own",
        3.0,
        scratch=[pltpu.VMEM((width, 2 * sz.slots), BF16)],
    )
    g_in = exchange(g_out)
    g_near = unpicked(g_in, "unpick_gradients", (gate_own,))
    b_rows, x_rows, g_rows = gather(b_near), gather(x_near), gather(g_near)

    hidden_f32 = ((sz.hidden, sz.slots), F32)
    hidden_bf16 = ((sz.slots, sz.hidden), BF16)
    (dh_own,) = near(
        part(hidden_gradient_own_kernel, sz),
        [hidden_f32],
        (g_near, wd),
        "hidden_gradient_own",
        1.0,
        scratch=[pltpu.VMEM((width, sz.slots), BF16)],
    )
    gate, up, hidden, *made = near(
        part(first_kernel, sz),
        [hidden_f32] * 2 + [hidden_bf16] + [rows] * (split - 1),
        (*b_rows[1:], *x_rows[1:], gate_own, up_own, wg, wu, wd),
        "first",
        4.0,
        scratch=[pltpu.VMEM((width, 2 * sz.slots), BF16), pltpu.VMEM(both, F32), pltpu.VMEM(both, F32)],
        after=(dh_own,),
    )
    made_in = scatter(made)
    d_gate, d_up, *back = near(
        part(backward_kernel, sz),
        [hidden_bf16] * 2 + [rows] * (split - 1),
        (*g_rows[1:], dh_own, gate, up, wg, wu, wd),
        "backward",
        3.0,
        scratch=[pltpu.VMEM((width, sz.slots), BF16), pltpu.VMEM((sz.hidden, sz.slots), F32)],
    )
    back_in = scatter(back)
    made_own = near(part(forward_own_kernel, sz), [rows], (hidden, wd), "forward_own", 1.0, after=(d_gate,))
    made_pieces = near(part(fold_kernel, sz), pieces, (*made_own, *made_in), "fold_forward")
    back_own = near(
        part(backward_own_kernel, sz), [rows], (d_gate, d_up, wg, wu), "backward_own", 1.5, after=made_pieces[:1]
    )
    made_pieces = exchange(made_pieces)
    back_pieces = exchange(near(part(fold_kernel, sz), pieces, (*back_own, *back_in), "fold_backward"))

    combine = lambda copies, args, name, after: near(
        part(combine_kernel, sz, copies),
        [block],
        args,
        name,
        1.2,
        scratch=[block_scratch, pltpu.SemaphoreType.DMA((sz.parts,))],
        after=after,
        far_outs=True,
    )[0]
    section_out = combine(2, (x_full, f_turned, *made_pieces), "combine_acts", back_pieces[:1])
    input_grads = combine(1, (dy_full, b_turned, *back_pieces), "combine_gradients", ())
    return (section_out[None], input_grads[None])


def solution(mesh):
    return jax.shard_map(
        shards,
        mesh=mesh,
        in_specs=(
            P("section", "expert", None),
            P("section", "expert", None),
            P("section", "expert", None),
            P("section", None, None),
            P("section", None, None),
            P("section", None, None),
            P("section", None, None),
            P("section", "expert", None),
            P("section", "expert", None),
            P("section", "expert", None),
        ),
        out_specs=(P("section", "expert", None), P("section", "expert", None)),
        check_vma=False,
    )
```

```python
import functools
import jax
import jax.numpy as jnp
from jax import lax
from jax.experimental import pallas as pl
from jax.experimental.pallas import tpu as pltpu
from jax.sharding import PartitionSpec as P

N_ROUTED = 256
TOP = 8
E_WIN = 4
F32 = jnp.float32
BF16 = jnp.bfloat16
VMEM_LIMIT = 8 << 20


def mm(a, b, ca=1, cb=0, precision=None):
    dims = (((ca,), (cb,)), ((), ()))
    return lax.dot_general(a, b, dims, precision=precision, preferred_element_type=F32)


class Sizes:
    def __init__(self, count, width, hidden, split):
        self.count, self.width, self.hidden, self.split = count, width, hidden, split
        self.cap = count * TOP * 2 // N_ROUTED
        self.slots = E_WIN * self.cap
        self.parts = min(4, width // 128)
        self.cols = width // self.parts
        self.piece = self.parts * self.cap
        self.spread = E_WIN * self.piece


def place_of(sz, i):
    piece = sum([(i >= sz.piece * n).astype(jnp.int32) for n in range(1, E_WIN)])
    i = i - sz.piece * piece
    part = sum([(i >= sz.cap * n).astype(jnp.int32) for n in range(1, sz.parts)])
    return piece, part, i - sz.cap * part


def one_hot(mask):
    return jnp.where(mask, 1.0, 0.0).astype(BF16)


def route_masks(routes, probs, expert, place, earlier):
    chosen = jnp.zeros(expert.shape, F32)
    weight = jnp.zeros(expert.shape, F32)
    for c in range(TOP):
        hit = routes[c : c + 1, :] == expert
        chosen += jnp.where(hit, 1.0, 0.0)
        if probs is not None:
            weight += jnp.where(hit, probs[c : c + 1, :], 0.0)
    before = mm(chosen.astype(BF16), earlier)
    mask = (chosen > 0.5) & (jnp.abs(before - place.astype(F32)) < 0.5)
    return mask, weight


def my_group(ref, group, count):
    block = ref[:, :count]
    for n in range(1, E_WIN):
        block = jnp.where(group == n, ref[:, n * count : (n + 1) * count], block)
    return block


def earlier_tokens(sz):
    shape = (sz.count, sz.count)
    return one_hot(lax.broadcasted_iota(jnp.int32, shape, 0) < lax.broadcasted_iota(jnp.int32, shape, 1))


def piece_masks(sz, routes_ref, probs_ref):
    group = lax.axis_index("expert") // sz.split
    shape = (sz.spread, sz.count)
    piece, part, place = place_of(sz, lax.broadcasted_iota(jnp.int32, shape, 0))
    routes = my_group(routes_ref, group, sz.count)
    probs = None if probs_ref is None else my_group(probs_ref, group, sz.count)
    mask, weight = route_masks(routes, probs, piece ^ group, place, earlier_tokens(sz))
    return mask, weight, part


def pick(sz, mask, part, values):
    picked = jnp.zeros((sz.spread, sz.cols), F32)
    for q in range(sz.parts):
        picked += mm(one_hot(mask & (part == q)), values[:, q * sz.cols : (q + 1) * sz.cols])
    return picked


def put_pieces(values, outs):
    step = values.shape[0] // len(outs)
    for n, out in enumerate(outs):
        out[...] = values[n * step : (n + 1) * step].astype(BF16)


def fetch(pairs, sems):
    copies = [pltpu.make_async_copy(src, dst, sems.at[n]) for n, (src, dst) in enumerate(pairs)]
    for c in copies:
        c.start()
    return copies


def local_kernel(sz, fr, fp, br, bp, saved, w_f, m_f, m_b, scale, *rest):
    pieces, (fr_v, fp_v, br_v, bp_v, saved_v, sems) = rest[:E_WIN], rest[E_WIN:]
    pairs = [(br, br_v), (bp, bp_v), (fr, fr_v), (fp, fp_v), (saved, saved_v)]
    copies = fetch(pairs, sems)
    for c in copies[:4]:
        c.wait()
    mask, weight, part = piece_masks(sz, br_v, bp_v)
    m_b[...] = one_hot(mask)
    total = jnp.sum(jnp.where(mask, weight, 0.0), axis=1, keepdims=True)
    scale[...] = jnp.broadcast_to(total, scale.shape)
    copies[4].wait()
    put_pieces(pick(sz, mask, part, saved_v), pieces)
    mask, weight, _ = piece_masks(sz, fr_v, fp_v)
    m_f[...] = one_hot(mask)
    w_f[...] = jnp.where(mask, weight, 0.0)


def pick_again_kernel(sz, scaled, chosen, *refs):
    values, pieces = refs[scaled], refs[scaled + 1 :]
    _, part, _ = place_of(sz, lax.broadcasted_iota(jnp.int32, (sz.spread, sz.count), 0))
    picked = pick(sz, chosen[...].astype(F32) > 0.5, part, values)
    put_pieces(picked * refs[0][:, 0:1] if scaled else picked, pieces)


def end_to_end(sz, pieces):
    if len(pieces) == E_WIN:
        return jnp.concatenate([p[...] for p in (pieces[0], *pieces[:0:-1])], axis=0)
    n = sz.piece
    low, high, relayed = pieces
    return jnp.concatenate([low[:n], relayed[:n], high[:n], relayed[n:]], axis=0)


def relay_kernel(sz, low, high, out):
    out[: sz.piece] = low[sz.piece :]
    out[sz.piece :] = high[sz.piece :]


def unpick(sz, cat, rows):
    shape = (sz.slots, sz.spread)
    slot = lax.broadcasted_iota(jnp.int32, shape, 0)
    piece, part, place = place_of(sz, lax.broadcasted_iota(jnp.int32, shape, 1))
    here = slot == piece * sz.cap + place
    for q in range(sz.parts):
        rows[:, q * sz.cols : (q + 1) * sz.cols] = mm(one_hot(here & (part == q)), cat).astype(BF16)


def unpick_kernel(sz, *refs):
    unpick(sz, end_to_end(sz, refs[:-1]), refs[-1])


def fold_kernel(sz, *refs):
    slices, pieces = refs[: sz.split], refs[sz.split :]
    rows = slices[0][...].astype(F32)
    for s in slices[1:]:
        rows += s[...].astype(F32)
    rows = rows.astype(BF16)
    shape = (sz.spread, sz.slots)
    piece, part, place = place_of(sz, lax.broadcasted_iota(jnp.int32, shape, 0))
    here = lax.broadcasted_iota(jnp.int32, shape, 1) == piece * sz.cap + place
    out = jnp.zeros((sz.spread, sz.cols), F32)
    for q in range(sz.parts):
        out += mm(one_hot(here & (part == q)), rows[:, q * sz.cols : (q + 1) * sz.cols])
    put_pieces(out, pieces)


def token_kernel(token):
    token[...] = jnp.zeros_like(token)


def combine(sz, copies, values, w, pieces, out, done, sems):
    cat = end_to_end(sz, pieces)
    stores = []
    for q in range(sz.parts):
        columns = pl.ds(q * sz.cols, sz.cols)
        total = values[:, columns].astype(F32)
        for n in range(copies):
            total += mm(w[q * copies + n], cat)
        done[:, columns] = total.astype(BF16)
        stores.append(pltpu.make_async_copy(done.at[:, columns], out.at[:, columns], sems.at[q]))
        stores[-1].start()
    return stores


def combine_kernel(sz, dy, w_b, x, w_f, *refs):
    (low, high, relayed), back, refs = refs[:3], refs[3 : E_WIN + 3], refs[E_WIN + 3 :]
    x_out, dy_out, dy_done, x_done, dy_sems, x_sems = refs
    stores = combine(sz, 1, dy, w_b, back, dy_out, dy_done, dy_sems)
    stores += combine(sz, 2, x, w_f, (low, high, relayed), x_out, x_done, x_sems)
    for store in stores:
        store.wait()


def turn_kernel(sz, w_f, w_b, f_turned, b_turned):
    _, part, _ = place_of(sz, lax.broadcasted_iota(jnp.int32, (sz.count, sz.spread), 1))
    f = w_f[...].T
    b = w_b[...].astype(F32).T
    for q in range(sz.parts):
        mine = jnp.where(part == q, f, 0.0)
        high = mine.astype(BF16)
        f_turned[2 * q] = high
        f_turned[2 * q + 1] = (mine - high.astype(F32)).astype(BF16)
        b_turned[q] = jnp.where(part == q, b, 0.0).astype(BF16)


def add_product(sz, weight, behind, turned, before, out):
    at = lax.rem(lax.axis_index("expert") + sz.split - behind, sz.split) * sz.width
    columns = pl.ds(pl.multiple_of(at, 128), sz.width)
    half = weight.shape[0] // 2
    for cut in (slice(0, half), slice(half, None)):
        product = mm(weight[cut, columns], turned[...])
        out[cut, :] = product if before is None else before[cut, :] + product


def turn(above, below):
    return jnp.concatenate([above[...], below[...]], axis=0).T


def first_own_kernel(sz, b, x, wg, wu, gate, up, turned):
    turned[...] = turn(b, x)
    add_product(sz, wg, 0, turned, None, gate)
    add_product(sz, wu, 0, turned, None, up)


def first_kernel(sz, *refs):
    n, m = sz.split - 1, sz.slots
    b_slices, x_slices, (gate_own, up_own, wg, wu, wd), refs = refs[:n], refs[n : 2 * n], refs[2 * n : 2 * n + 5], refs[2 * n + 5 :]
    gate, up, hidden, *outs = refs[:-1]
    turned = refs[-1]
    for j, (b, x) in enumerate(zip(b_slices, x_slices)):
        turned[...] = turn(b, x)
        add_product(sz, wg, j + 1, turned, gate_own if j == 0 else gate, gate)
        add_product(sz, wu, j + 1, turned, up_own if j == 0 else up, up)
    g = gate[...]
    hidden[...] = (g * jax.nn.sigmoid(g) * up[...]).T[m:].astype(BF16)
    forward_slices(sz, range(1, sz.split), hidden, wd, outs)


def columns_of(sz, j):
    me = lax.rem(lax.axis_index("expert"), sz.split)
    at = lax.rem(me + j, sz.split) * sz.width
    block = min(512, sz.width)
    return [
        (pl.ds(n * block, block), pl.ds(pl.multiple_of(at + n * block, 128), block))
        for n in range(sz.width // block)
    ]


def backward_slices(sz, js, d_gate, d_up, wg, wu, outs):
    for j, out in zip(js, outs):
        for here, there in columns_of(sz, j):
            out[:, here] = (mm(d_gate[...], wg[:, there]) + mm(d_up[...], wu[:, there])).astype(BF16)


def forward_slices(sz, js, hidden, wd, outs):
    for j, out in zip(js, outs):
        for here, there in columns_of(sz, j):
            out[:, here] = mm(hidden[...], wd[:, there]).astype(BF16)


def hidden_gradient_own_kernel(sz, g, wd, dh, turned):
    turned[...] = g[...].T
    add_product(sz, wd, 0, turned, None, dh)


def backward_kernel(sz, *refs):
    n = sz.split - 1
    slices, (dh_own, gate, up, wg, wu, wd), refs = refs[:n], refs[n : n + 6], refs[n + 6 :]
    d_gate, d_up, *outs = refs[:-2]
    turned, dh_all = refs[-2:]
    for j, s in enumerate(slices):
        turned[...] = s[...].T
        add_product(sz, wd, j + 1, turned, dh_own if j == 0 else dh_all, dh_all)
    dh = dh_all[...]
    g = gate[:, : sz.slots]
    sig = jax.nn.sigmoid(g)
    d_up[...] = (dh * (g * sig)).T.astype(BF16)
    d_gate[...] = (dh * up[:, : sz.slots] * sig * (1.0 + g * (1.0 - sig))).T.astype(BF16)
    backward_slices(sz, range(1, sz.split), d_gate, d_up, wg, wu, outs)


def backward_own_kernel(sz, d_gate, d_up, wg, wu, out):
    backward_slices(sz, (0,), d_gate, d_up, wg, wu, (out,))


def forward_own_kernel(sz, hidden, wd, out):
    forward_slices(sz, (0,), hidden, wd, (out,))


def near(kernel, outs, args, name, us=0.3, far=(), scratch=(), after=(), far_outs=False):
    spaces = [pltpu.HBM if i in far else pltpu.VMEM for i in range(len(args))] + [pl.ANY] * len(after)
    args = [pltpu.with_memory_space_constraint(a, pltpu.HBM) if i in far else a for i, a in enumerate(args)]

    def body(*refs):
        kernel(*refs[: len(args)], *refs[len(args) + len(after) :])

    return pl.pallas_call(
        body,
        out_shape=[jax.ShapeDtypeStruct(s, d) for s, d in outs],
        name=name,
        in_specs=[pl.BlockSpec(memory_space=s) for s in spaces],
        out_specs=[pl.BlockSpec(memory_space=pltpu.HBM if far_outs else pltpu.VMEM) for _ in outs],
        scratch_shapes=list(scratch),
        compiler_params=pltpu.CompilerParams(vmem_limit_bytes=VMEM_LIMIT),
        cost_estimate=pl.CostEstimate(flops=int(us * 1.1e9), bytes_accessed=1 << 16, transcendentals=0),
    )(*args, *after)


def shards(
    section_acts,
    section_input_gradients,
    saved_input,
    fwd_routes,
    fwd_probs,
    back_routes,
    back_probs,
    w_gate,
    w_up,
    w_down,
):
    experts = lax.axis_size("expert")
    sections = lax.axis_size("section")
    split = experts // E_WIN
    acts, grads, saved = section_acts[0], section_input_gradients[0], saved_input[0]
    wg, wu, wd = w_gate[0], w_up[0], w_down[0]
    count, width = acts.shape
    sz = Sizes(count, width, wg.shape[0], split)
    full = width * split
    piece = ((sz.piece, sz.cols), BF16)
    rows = ((sz.slots, width), BF16)

    def by_section(x, by):
        return lax.ppermute(x, "section", [(i, (i + by) % sections) for i in range(sections)])

    def exchange(pieces):
        pairs = lambda o: [(e, (e // split ^ o) * split + e % split) for e in range(experts)]
        return [pieces[0]] + [lax.ppermute(pieces[o], "expert", pairs(o)) for o in range(E_WIN - 1, 0, -1)]

    def exchange_by_halves(low, high, after):
        send = lambda x, o: lax.ppermute(x, "expert", [(e, (e // split ^ o) * split + e % split) for e in range(experts)])
        high = send(high, 2)
        relay = near(functools.partial(relay_kernel, sz), [(low.shape, BF16)], (low, high), "relay", 0.1, after=after)
        return low, high, relay[0], lambda x: send(x, 1)

    def along_group(x, by):
        pairs = [(e, e // split * split + (e + by) % split) for e in range(experts)]
        return lax.ppermute(x, "expert", pairs)

    def gather(x):
        return [x] + [along_group(x, j) for j in range(1, split)]

    def scatter(slices):
        return tuple(along_group(s, j) for j, s in enumerate(slices, 1))

    part = functools.partial
    pieces = [piece] * E_WIN
    block = ((count, width), BF16)
    held = ((sz.spread, sz.cols), BF16)
    route_scratch = [pltpu.VMEM(fwd_routes.shape[:0:-1], d) for d in (jnp.int32, F32)]
    block_scratch = pltpu.VMEM((count, width), BF16)

    fr, fp, br, bp = fwd_routes[0].T, fwd_probs[0].T, back_routes[0].T, back_probs[0].T
    x_full = by_section(acts, 1)
    table = (sz.spread, count)
    w_f, m_f, m_b, scale, *b_out = near(
        part(local_kernel, sz),
        [(table, F32), (table, BF16), (table, BF16), ((sz.spread, 128), F32)] + pieces,
        (fr, fp, br, bp, saved),
        "local",
        2.0,
        far=range(5),
        scratch=route_scratch * 2 + [block_scratch, pltpu.SemaphoreType.DMA((5,))],
    )
    b_in = exchange(b_out)
    grads, m_b = lax.optimization_barrier((grads, m_b))
    dy_full = by_section(grads, -1)
    f_turned, b_turned = near(
        part(turn_kernel, sz), [((n * sz.parts, count, sz.spread), BF16) for n in (2, 1)], (w_f, m_b), "turn", 4.0
    )
    unpicked = lambda pieces, name, after=(): near(part(unpick_kernel, sz), [rows], pieces, name, after=after)[0]
    b_near = unpicked(b_in, "unpick_saved", (f_turned,))
    x_out = near(part(pick_again_kernel, sz, 0), pieces, (m_f, x_full), "pick_acts", 4.5, after=(b_near,))
    x_in = exchange(x_out)
    g_out = near(
        part(pick_again_kernel, sz, 1), pieces, (m_b, scale, dy_full), "pick_gradients", 0.5, after=x_out[:1]
    )
    x_near = unpicked(x_in, "unpick_acts", g_out[:1])
    both = (sz.hidden, 2 * sz.slots)
    gate_own, up_own = near(
        part(first_own_kernel, sz),
        [(both, F32)] * 2,
        (b_near, x_near, wg, wu),
        "first_own",
        3.0,
        scratch=[pltpu.VMEM((width, 2 * sz.slots), BF16)],
    )
    g_in = exchange(g_out)
    g_near = unpicked(g_in, "unpick_gradients", (gate_own,))
    b_rows, x_rows, g_rows = gather(b_near), gather(x_near), gather(g_near)

    hidden_f32 = ((sz.hidden, sz.slots), F32)
    hidden_bf16 = ((sz.slots, sz.hidden), BF16)
    (dh_own,) = near(
        part(hidden_gradient_own_kernel, sz),
        [hidden_f32],
        (g_near, wd),
        "hidden_gradient_own",
        1.0,
        scratch=[pltpu.VMEM((width, sz.slots), BF16)],
    )
    gate, up, hidden, *made = near(
        part(first_kernel, sz),
        [(both, F32)] * 2 + [hidden_bf16] + [rows] * (split - 1),
        (*b_rows[1:], *x_rows[1:], gate_own, up_own, wg, wu, wd),
        "first",
        4.0,
        scratch=[pltpu.VMEM((width, 2 * sz.slots), BF16)],
        after=(dh_own,),
    )
    made_in = scatter(made)
    d_gate, d_up, *back = near(
        part(backward_kernel, sz),
        [hidden_bf16] * 2 + [rows] * (split - 1),
        (*g_rows[1:], dh_own, gate, up, wg, wu, wd),
        "backward",
        3.0,
        scratch=[pltpu.VMEM((width, sz.slots), BF16), pltpu.VMEM((sz.hidden, sz.slots), F32)],
    )
    back_in = scatter(back)
    made_own = near(part(forward_own_kernel, sz), [rows], (hidden, wd), "forward_own", 1.0, after=(d_gate,))
    half = ((2 * sz.piece, sz.cols), BF16)
    made_halves = near(part(fold_kernel, sz), [half, half], (*made_own, *made_in), "fold_forward")
    back_own = near(
        part(backward_own_kernel, sz), [rows], (d_gate, d_up, wg, wu), "backward_own", 1.5, after=made_halves[:1]
    )
    back_pieces = near(part(fold_kernel, sz), pieces, (*back_own, *back_in), "fold_backward")
    low, high, relay, send_on = exchange_by_halves(*made_halves, back_pieces[:1])
    last, relay = lax.optimization_barrier((back_pieces[1], relay))
    back_pieces = exchange([back_pieces[0], last, *back_pieces[2:]])
    made_pieces = (low, high, send_on(relay))
    (arrived,) = near(token_kernel, [((8, 128), F32)], (), "arrived", 1.2, after=back_pieces[1:3])
    section_out, input_grads = near(
        part(combine_kernel, sz),
        [block, block],
        (dy_full, b_turned, x_full, f_turned, *made_pieces, *back_pieces),
        "combine",
        2.0,
        scratch=[block_scratch, block_scratch] + [pltpu.SemaphoreType.DMA((sz.parts,))] * 2,
        far_outs=True,
        after=(arrived,),
    )
    return (section_out[None], input_grads[None])


def solution(mesh):
    return jax.shard_map(
        shards,
        mesh=mesh,
        in_specs=(
            P("section", "expert", None),
            P("section", "expert", None),
            P("section", "expert", None),
            P("section", None, None),
            P("section", None, None),
            P("section", None, None),
            P("section", None, None),
            P("section", "expert", None),
            P("section", "expert", None),
            P("section", "expert", None),
        ),
        out_specs=(P("section", "expert", None), P("section", "expert", None)),
        check_vma=False,
    )
```

```python
import functools
import jax
import jax.numpy as jnp
from jax import lax
from jax.experimental import pallas as pl
from jax.experimental.pallas import tpu as pltpu
from jax.sharding import PartitionSpec as P

N_ROUTED = 256
TOP = 8
E_WIN = 4
F32 = jnp.float32
BF16 = jnp.bfloat16
VMEM_LIMIT = 8 << 20


def mm(a, b, ca=1, cb=0, precision=None):
    dims = (((ca,), (cb,)), ((), ()))
    return lax.dot_general(a, b, dims, precision=precision, preferred_element_type=F32)


class Sizes:
    def __init__(self, count, width, hidden, split):
        self.count, self.width, self.hidden, self.split = count, width, hidden, split
        self.cap = count * TOP * 2 // N_ROUTED
        self.slots = E_WIN * self.cap
        self.parts = min(4, width // 128)
        self.cols = width // self.parts
        self.piece = self.parts * self.cap
        self.spread = E_WIN * self.piece


def place_of(sz, i):
    piece = sum([(i >= sz.piece * n).astype(jnp.int32) for n in range(1, E_WIN)])
    i = i - sz.piece * piece
    part = sum([(i >= sz.cap * n).astype(jnp.int32) for n in range(1, sz.parts)])
    return piece, part, i - sz.cap * part


def one_hot(mask):
    return jnp.where(mask, 1.0, 0.0).astype(BF16)


def route_masks(routes, probs, expert, place, earlier):
    chosen = jnp.zeros(expert.shape, F32)
    weight = jnp.zeros(expert.shape, F32)
    for c in range(TOP):
        hit = routes[c : c + 1, :] == expert
        chosen += jnp.where(hit, 1.0, 0.0)
        if probs is not None:
            weight += jnp.where(hit, probs[c : c + 1, :], 0.0)
    before = mm(chosen.astype(BF16), earlier)
    mask = (chosen > 0.5) & (jnp.abs(before - place.astype(F32)) < 0.5)
    return mask, weight


def my_group(ref, group, count):
    block = ref[:, :count]
    for n in range(1, E_WIN):
        block = jnp.where(group == n, ref[:, n * count : (n + 1) * count], block)
    return block


def earlier_tokens(sz):
    shape = (sz.count, sz.count)
    return one_hot(lax.broadcasted_iota(jnp.int32, shape, 0) < lax.broadcasted_iota(jnp.int32, shape, 1))


def piece_masks(sz, routes_ref, probs_ref):
    group = lax.axis_index("expert") // sz.split
    shape = (sz.spread, sz.count)
    piece, part, place = place_of(sz, lax.broadcasted_iota(jnp.int32, shape, 0))
    routes = my_group(routes_ref, group, sz.count)
    probs = None if probs_ref is None else my_group(probs_ref, group, sz.count)
    mask, weight = route_masks(routes, probs, piece ^ group, place, earlier_tokens(sz))
    return mask, weight, part


def pick(sz, mask, part, values):
    picked = jnp.zeros((sz.spread, sz.cols), F32)
    for q in range(sz.parts):
        picked += mm(one_hot(mask & (part == q)), values[:, q * sz.cols : (q + 1) * sz.cols])
    return picked


def put_pieces(values, outs):
    step = values.shape[0] // len(outs)
    for n, out in enumerate(outs):
        out[...] = values[n * step : (n + 1) * step].astype(BF16)


def fetch(pairs, sems):
    copies = [pltpu.make_async_copy(src, dst, sems.at[n]) for n, (src, dst) in enumerate(pairs)]
    for c in copies:
        c.start()
    return copies


def local_kernel(sz, fr, fp, br, bp, saved, w_f, m_f, m_b, scale, *rest):
    pieces, (fr_v, fp_v, br_v, bp_v, saved_v, sems) = rest[:E_WIN], rest[E_WIN:]
    pairs = [(br, br_v), (bp, bp_v), (fr, fr_v), (fp, fp_v), (saved, saved_v)]
    copies = fetch(pairs, sems)
    for c in copies[:4]:
        c.wait()
    mask, weight, part = piece_masks(sz, br_v, bp_v)
    m_b[...] = one_hot(mask)
    total = jnp.sum(jnp.where(mask, weight, 0.0), axis=1, keepdims=True)
    scale[...] = jnp.broadcast_to(total, scale.shape)
    copies[4].wait()
    put_pieces(pick(sz, mask, part, saved_v), pieces)
    mask, weight, _ = piece_masks(sz, fr_v, fp_v)
    m_f[...] = one_hot(mask)
    w_f[...] = jnp.where(mask, weight, 0.0)


def pick_again_kernel(sz, scaled, chosen, *refs):
    values, pieces = refs[scaled], refs[scaled + 1 :]
    _, part, _ = place_of(sz, lax.broadcasted_iota(jnp.int32, (sz.spread, sz.count), 0))
    picked = pick(sz, chosen[...].astype(F32) > 0.5, part, values)
    put_pieces(picked * refs[0][:, 0:1] if scaled else picked, pieces)


def end_to_end(sz, pieces):
    if len(pieces) == E_WIN:
        return jnp.concatenate([p[...] for p in (pieces[0], *pieces[:0:-1])], axis=0)
    n = sz.piece
    low, high, relayed = pieces
    return jnp.concatenate([low[:n], relayed[:n], high[:n], relayed[n:]], axis=0)


def relay_kernel(sz, low, high, back, out):
    n = sz.piece
    out[:n] = low[n:]
    out[n : 2 * n] = high[n:]
    out[2 * n :] = back[...]


def unpick(sz, cat, rows):
    shape = (sz.slots, sz.spread)
    slot = lax.broadcasted_iota(jnp.int32, shape, 0)
    piece, part, place = place_of(sz, lax.broadcasted_iota(jnp.int32, shape, 1))
    here = slot == piece * sz.cap + place
    for q in range(sz.parts):
        rows[:, q * sz.cols : (q + 1) * sz.cols] = mm(one_hot(here & (part == q)), cat).astype(BF16)


def unpick_kernel(sz, *refs):
    unpick(sz, end_to_end(sz, refs[:-1]), refs[-1])


def fold_kernel(sz, *refs):
    slices, pieces = refs[: sz.split], refs[sz.split :]
    rows = slices[0][...].astype(F32)
    for s in slices[1:]:
        rows += s[...].astype(F32)
    rows = rows.astype(BF16)
    shape = (sz.spread, sz.slots)
    piece, part, place = place_of(sz, lax.broadcasted_iota(jnp.int32, shape, 0))
    here = lax.broadcasted_iota(jnp.int32, shape, 1) == piece * sz.cap + place
    out = jnp.zeros((sz.spread, sz.cols), F32)
    for q in range(sz.parts):
        out += mm(one_hot(here & (part == q)), rows[:, q * sz.cols : (q + 1) * sz.cols])
    put_pieces(out, pieces)


def token_kernel(token):
    token[...] = jnp.zeros_like(token)


def combine(sz, copies, values, w, pieces, out, done, sems):
    cat = jnp.concatenate(pieces, axis=0)
    stores = []
    for q in range(sz.parts):
        columns = pl.ds(q * sz.cols, sz.cols)
        total = values[:, columns].astype(F32)
        for n in range(copies):
            total += mm(w[q * copies + n], cat)
        done[:, columns] = total.astype(BF16)
        stores.append(pltpu.make_async_copy(done.at[:, columns], out.at[:, columns], sems.at[q]))
        stores[-1].start()
    return stores


def combine_kernel(sz, dy, w_b, x, w_f, *refs):
    own, far, mid, low, high, relayed = refs[:6]
    x_out, dy_out, dy_done, x_done, dy_sems, x_sems = refs[6:]
    n = sz.piece
    back = (own[...], relayed[2 * n :], mid[...], far[...])
    made = (low[:n], relayed[:n], high[:n], relayed[n : 2 * n])
    stores = combine(sz, 1, dy, w_b, back, dy_out, dy_done, dy_sems)
    stores += combine(sz, 2, x, w_f, made, x_out, x_done, x_sems)
    for store in stores:
        store.wait()


def turn_kernel(sz, w_f, w_b, f_turned, b_turned):
    _, part, _ = place_of(sz, lax.broadcasted_iota(jnp.int32, (sz.count, sz.spread), 1))
    f = w_f[...].T
    b = w_b[...].astype(F32).T
    for q in range(sz.parts):
        mine = jnp.where(part == q, f, 0.0)
        high = mine.astype(BF16)
        f_turned[2 * q] = high
        f_turned[2 * q + 1] = (mine - high.astype(F32)).astype(BF16)
        b_turned[q] = jnp.where(part == q, b, 0.0).astype(BF16)


def add_product(sz, weight, behind, turned, before, out):
    at = lax.rem(lax.axis_index("expert") + sz.split - behind, sz.split) * sz.width
    columns = pl.ds(pl.multiple_of(at, 128), sz.width)
    half = weight.shape[0] // 2
    for cut in (slice(0, half), slice(half, None)):
        product = mm(weight[cut, columns], turned[...])
        out[cut, :] = product if before is None else before[cut, :] + product


def turn(above, below):
    return jnp.concatenate([above[...], below[...]], axis=0).T


def first_own_kernel(sz, b, x, wg, wu, gate, up, turned):
    turned[...] = turn(b, x)
    add_product(sz, wg, 0, turned, None, gate)
    add_product(sz, wu, 0, turned, None, up)


def first_kernel(sz, *refs):
    n, m = sz.split - 1, sz.slots
    b_slices, x_slices, (gate_own, up_own, wg, wu, wd), refs = refs[:n], refs[n : 2 * n], refs[2 * n : 2 * n + 5], refs[2 * n + 5 :]
    gate, up, hidden, *outs = refs[:-1]
    turned = refs[-1]
    for j, (b, x) in enumerate(zip(b_slices, x_slices)):
        turned[...] = turn(b, x)
        add_product(sz, wg, j + 1, turned, gate_own if j == 0 else gate, gate)
        add_product(sz, wu, j + 1, turned, up_own if j == 0 else up, up)
    g = gate[...]
    hidden[...] = (g * jax.nn.sigmoid(g) * up[...]).T[m:].astype(BF16)
    forward_slices(sz, range(1, sz.split), hidden, wd, outs)


def columns_of(sz, j):
    me = lax.rem(lax.axis_index("expert"), sz.split)
    at = lax.rem(me + j, sz.split) * sz.width
    block = min(512, sz.width)
    return [
        (pl.ds(n * block, block), pl.ds(pl.multiple_of(at + n * block, 128), block))
        for n in range(sz.width // block)
    ]


def backward_slices(sz, js, d_gate, d_up, wg, wu, outs):
    for j, out in zip(js, outs):
        for here, there in columns_of(sz, j):
            out[:, here] = (mm(d_gate[...], wg[:, there]) + mm(d_up[...], wu[:, there])).astype(BF16)


def forward_slices(sz, js, hidden, wd, outs):
    for j, out in zip(js, outs):
        for here, there in columns_of(sz, j):
            out[:, here] = mm(hidden[...], wd[:, there]).astype(BF16)


def hidden_gradient_own_kernel(sz, g, wd, dh, turned):
    turned[...] = g[...].T
    add_product(sz, wd, 0, turned, None, dh)


def backward_kernel(sz, *refs):
    n = sz.split - 1
    slices, (dh_own, gate, up, wg, wu, wd), refs = refs[:n], refs[n : n + 6], refs[n + 6 :]
    d_gate, d_up, *outs = refs[:-2]
    turned, dh_all = refs[-2:]
    for j, s in enumerate(slices):
        turned[...] = s[...].T
        add_product(sz, wd, j + 1, turned, dh_own if j == 0 else dh_all, dh_all)
    dh = dh_all[...]
    g = gate[:, : sz.slots]
    sig = jax.nn.sigmoid(g)
    d_up[...] = (dh * (g * sig)).T.astype(BF16)
    d_gate[...] = (dh * up[:, : sz.slots] * sig * (1.0 + g * (1.0 - sig))).T.astype(BF16)
    backward_slices(sz, range(1, sz.split), d_gate, d_up, wg, wu, outs)


def backward_own_kernel(sz, d_gate, d_up, wg, wu, out):
    backward_slices(sz, (0,), d_gate, d_up, wg, wu, (out,))


def forward_own_kernel(sz, hidden, wd, out):
    forward_slices(sz, (0,), hidden, wd, (out,))


def near(kernel, outs, args, name, us=0.3, far=(), scratch=(), after=(), far_outs=False):
    spaces = [pltpu.HBM if i in far else pltpu.VMEM for i in range(len(args))] + [pl.ANY] * len(after)
    args = [pltpu.with_memory_space_constraint(a, pltpu.HBM) if i in far else a for i, a in enumerate(args)]

    def body(*refs):
        kernel(*refs[: len(args)], *refs[len(args) + len(after) :])

    return pl.pallas_call(
        body,
        out_shape=[jax.ShapeDtypeStruct(s, d) for s, d in outs],
        name=name,
        in_specs=[pl.BlockSpec(memory_space=s) for s in spaces],
        out_specs=[pl.BlockSpec(memory_space=pltpu.HBM if far_outs else pltpu.VMEM) for _ in outs],
        scratch_shapes=list(scratch),
        compiler_params=pltpu.CompilerParams(vmem_limit_bytes=VMEM_LIMIT),
        cost_estimate=pl.CostEstimate(flops=int(us * 1.1e9), bytes_accessed=1 << 16, transcendentals=0),
    )(*args, *after)


def shards(
    section_acts,
    section_input_gradients,
    saved_input,
    fwd_routes,
    fwd_probs,
    back_routes,
    back_probs,
    w_gate,
    w_up,
    w_down,
):
    experts = lax.axis_size("expert")
    sections = lax.axis_size("section")
    split = experts // E_WIN
    acts, grads, saved = section_acts[0], section_input_gradients[0], saved_input[0]
    wg, wu, wd = w_gate[0], w_up[0], w_down[0]
    count, width = acts.shape
    sz = Sizes(count, width, wg.shape[0], split)
    full = width * split
    piece = ((sz.piece, sz.cols), BF16)
    rows = ((sz.slots, width), BF16)

    def by_section(x, by):
        return lax.ppermute(x, "section", [(i, (i + by) % sections) for i in range(sections)])

    def send(x, o):
        return lax.ppermute(x, "expert", [(e, (e // split ^ o) * split + e % split) for e in range(experts)])

    def exchange(pieces):
        return [pieces[0]] + [send(pieces[o], o) for o in range(E_WIN - 1, 0, -1)]

    def along_group(x, by):
        pairs = [(e, e // split * split + (e + by) % split) for e in range(experts)]
        return lax.ppermute(x, "expert", pairs)

    def gather(x):
        return [x] + [along_group(x, j) for j in range(1, split)]

    def scatter(slices):
        return tuple(along_group(s, j) for j, s in enumerate(slices, 1))

    part = functools.partial
    pieces = [piece] * E_WIN
    block = ((count, width), BF16)
    held = ((sz.spread, sz.cols), BF16)
    route_scratch = [pltpu.VMEM(fwd_routes.shape[:0:-1], d) for d in (jnp.int32, F32)]
    block_scratch = pltpu.VMEM((count, width), BF16)

    fr, fp, br, bp = fwd_routes[0].T, fwd_probs[0].T, back_routes[0].T, back_probs[0].T
    x_full = by_section(acts, 1)
    table = (sz.spread, count)
    w_f, m_f, m_b, scale, *b_out = near(
        part(local_kernel, sz),
        [(table, F32), (table, BF16), (table, BF16), ((sz.spread, 128), F32)] + pieces,
        (fr, fp, br, bp, saved),
        "local",
        2.0,
        far=range(5),
        scratch=route_scratch * 2 + [block_scratch, pltpu.SemaphoreType.DMA((5,))],
    )
    b_in = exchange(b_out)
    grads, m_b = lax.optimization_barrier((grads, m_b))
    dy_full = by_section(grads, -1)
    f_turned, b_turned = near(
        part(turn_kernel, sz), [((n * sz.parts, count, sz.spread), BF16) for n in (2, 1)], (w_f, m_b), "turn", 4.0
    )
    unpicked = lambda pieces, name, after=(): near(part(unpick_kernel, sz), [rows], pieces, name, after=after)[0]
    b_near = unpicked(b_in, "unpick_saved", (f_turned,))
    x_out = near(part(pick_again_kernel, sz, 0), pieces, (m_f, x_full), "pick_acts", 4.5, after=(b_near,))
    x_in = exchange(x_out)
    g_out = near(
        part(pick_again_kernel, sz, 1), pieces, (m_b, scale, dy_full), "pick_gradients", 0.5, after=x_out[:1]
    )
    x_near = unpicked(x_in, "unpick_acts", g_out[:1])
    both = (sz.hidden, 2 * sz.slots)
    gate_own, up_own = near(
        part(first_own_kernel, sz),
        [(both, F32)] * 2,
        (b_near, x_near, wg, wu),
        "first_own",
        3.0,
        scratch=[pltpu.VMEM((width, 2 * sz.slots), BF16)],
    )
    g_in = exchange(g_out)
    g_near = unpicked(g_in, "unpick_gradients", (gate_own,))
    b_rows, x_rows, g_rows = gather(b_near), gather(x_near), gather(g_near)

    hidden_f32 = ((sz.hidden, sz.slots), F32)
    hidden_bf16 = ((sz.slots, sz.hidden), BF16)
    (dh_own,) = near(
        part(hidden_gradient_own_kernel, sz),
        [hidden_f32],
        (g_near, wd),
        "hidden_gradient_own",
        1.0,
        scratch=[pltpu.VMEM((width, sz.slots), BF16)],
    )
    gate, up, hidden, *made = near(
        part(first_kernel, sz),
        [(both, F32)] * 2 + [hidden_bf16] + [rows] * (split - 1),
        (*b_rows[1:], *x_rows[1:], gate_own, up_own, wg, wu, wd),
        "first",
        4.0,
        scratch=[pltpu.VMEM((width, 2 * sz.slots), BF16)],
        after=(dh_own,),
    )
    made_in = scatter(made)
    d_gate, d_up, *back = near(
        part(backward_kernel, sz),
        [hidden_bf16] * 2 + [rows] * (split - 1),
        (*g_rows[1:], dh_own, gate, up, wg, wu, wd),
        "backward",
        3.0,
        scratch=[pltpu.VMEM((width, sz.slots), BF16), pltpu.VMEM((sz.hidden, sz.slots), F32)],
    )
    back_in = scatter(back)
    made_own = near(part(forward_own_kernel, sz), [rows], (hidden, wd), "forward_own", 1.0, after=(d_gate,))
    half = ((2 * sz.piece, sz.cols), BF16)
    made_halves = near(part(fold_kernel, sz), [half, half], (*made_own, *made_in), "fold_forward")
    back_own = near(
        part(backward_own_kernel, sz), [rows], (d_gate, d_up, wg, wu), "backward_own", 1.5, after=made_halves[:1]
    )
    back_pieces = near(part(fold_kernel, sz), pieces, (*back_own, *back_in), "fold_backward")
    low, high = made_halves[0], send(made_halves[1], 2)
    back_far, back_mid = send(back_pieces[3], 3), send(back_pieces[2], 2)
    (relay,) = near(part(relay_kernel, sz), [((3 * sz.piece, sz.cols), BF16)], (low, high, back_pieces[1]), "relay", 0.1)
    relayed = send(relay, 1)
    (arrived,) = near(token_kernel, [((8, 128), F32)], (), "arrived", 3.0, after=(back_far, back_mid))
    section_out, input_grads = near(
        part(combine_kernel, sz),
        [block, block],
        (dy_full, b_turned, x_full, f_turned, back_pieces[0], back_far, back_mid, low, high, relayed),
        "combine",
        2.0,
        scratch=[block_scratch, block_scratch] + [pltpu.SemaphoreType.DMA((sz.parts,))] * 2,
        far_outs=True,
        after=(arrived,),
    )
    return (section_out[None], input_grads[None])


def solution(mesh):
    return jax.shard_map(
        shards,
        mesh=mesh,
        in_specs=(
            P("section", "expert", None),
            P("section", "expert", None),
            P("section", "expert", None),
            P("section", None, None),
            P("section", None, None),
            P("section", None, None),
            P("section", None, None),
            P("section", "expert", None),
            P("section", "expert", None),
            P("section", "expert", None),
        ),
        out_specs=(P("section", "expert", None), P("section", "expert", None)),
        check_vma=False,
    )
```
